32 devices in a mesh: blk: 16 (over z, y, core), rep: 2 (over x).
Axes of the slice: x: 2, y: 2, z: 4, core: 2. Of those that a mesh axis runs over, the one named last changes fastest.
Arguments:
- pooled: bfloat16 [2, 2048, 1536], P('rep', 'blk'), may hold values from -6 to 6
- w_img: bfloat16 [1536, 1024], replicated, may hold values from -0.15625 to 0.15625
- text_emb: bfloat16 [2, 2048, 1024], P('rep', 'blk'), may hold values from -6 to 6
- pos_index: int32 [2, 2048], P('rep', 'blk'), may hold values from 0 to 2047, each once within a row
- log_scale: float32 [1], replicated, may hold values from 1.5 to 2.5
- bias: float32 [1], replicated, may hold values from -2 to -0.5
Outputs:
- row_loss: float32 [2, 2048], P('rep', 'blk')
- weight_grad: float32 [1536, 1024], P(('blk', 'rep'))
- text_grad: float32 [2, 2048, 1024], P('rep', 'blk')
The draws below stay inside these ranges and needn't reach their ends.
Inputs may be any that keep to these rules, and one draw needn't show every extreme that they name: `pos_index`: each group's row is a permutation of 0 to 2047.
All inputs are finite; a program needn't handle non-finite values.
Results may differ from the reference program's by a relative error of at most 0.0052.
Values may be sent and summed in bfloat16 or wider, within the bound.
A program may use at most 192 MiB of HBM per device.

```python
import jax
import jax.numpy as jnp
from jax import lax

D_IMG = 1536
D_EMB = 1024
REPS = 2
BG = 2048


def level_of(own_key, extent, cuts, least, high):
    def one(dim, parts):
        draws = jax.random.uniform(jax.random.fold_in(jax.random.fold_in(own_key, 6), dim), (parts,), jnp.float32, least / len(cuts), high / len(cuts))
        return jnp.repeat(jnp.exp(draws), extent[dim] // parts).reshape((-1,) + (1,) * (len(extent) - dim - 1))

    gain = one(*cuts[0])
    for cut in cuts[1:]:
        gain = gain * one(*cut)
    return gain


def centred(stream_key, extent, spread, most, pieces=(), kind=jnp.bfloat16):
    array = jax.random.normal(stream_key, extent, jnp.float32) * spread
    if len(pieces) > 0:
        array = level_of(stream_key, extent, pieces, -0.22, 0.18) * array
    return jnp.clip(array, min=-most, max=most).astype(kind)


def setup_inputs(seed: int = 0) -> dict:
    streams_of = jax.random.split(jax.random.key(seed), 7)
    return {
        "pooled": centred(streams_of[0], (REPS, BG, D_IMG), 1.0, 6.0, ((0, 2), (1, 16))),
        "w_img": centred(streams_of[1], (D_IMG, D_EMB), D_IMG ** -0.5, 0.15625),
        "text_emb": centred(streams_of[2], (REPS, BG, D_EMB), 1.0, 6.0, ((0, 2), (1, 16))),
        "pos_index": jax.vmap(lambda own: jax.random.permutation(own, BG))(jax.random.split(streams_of[3], REPS)).reshape((REPS, BG)).astype(jnp.int32),
        "log_scale": jnp.clip(jax.random.uniform(streams_of[4], (1,), jnp.float32, 1.5, 2.5), 1.5, 2.5),
        "bias": jnp.clip(jax.random.uniform(streams_of[5], (1,), jnp.float32, -2.0, -0.5), -2.0, -0.5),
    }


def normalize(rows):
    squares = lax.optimization_barrier(jnp.sum(rows * rows, axis=-1, keepdims=True))
    inverse = lax.rsqrt(squares + 1e-06)
    return (rows * inverse, inverse)

def pair_terms(left, right, left_pos, right_start, scale_value, shift):
    logits = scale_value * jnp.dot(left, right.T, preferred_element_type=jnp.float32) + shift
    columns = right_start + jnp.arange(right.shape[0], dtype=jnp.int32)
    sign = jnp.where(left_pos[:, None] == columns[None, :], 1.0, -1.0).astype(logits.dtype)
    losses = jax.nn.softplus(-sign * logits)
    coeffs = (-sign * jax.nn.sigmoid(-sign * logits) * scale_value).astype(jnp.bfloat16)
    return (lax.optimization_barrier(jnp.sum(losses, axis=1)), coeffs)

def reference(pooled, w_img, text_emb, pos_index, log_scale, bias):
    scale_value = jnp.exp(log_scale[0])
    shift = bias[0]
    losses_all = []
    texts_all = []
    weight_total = jnp.zeros((D_IMG, D_EMB), jnp.float32)
    for group in range(REPS):
        features = pooled[group]
        projected = jnp.dot(features, w_img, preferred_element_type=jnp.float32)
        image_unit, image_inv = normalize(projected)
        image_low = image_unit.astype(jnp.bfloat16)
        text_unit, text_inv = normalize(text_emb[group].astype(jnp.float32))
        text_low = text_unit.astype(jnp.bfloat16)
        row_sums, coeffs = pair_terms(image_low, text_low, pos_index[group], 0, scale_value, shift)
        image_dir = jnp.dot(coeffs, text_low, preferred_element_type=jnp.float32)
        text_dir = jnp.dot(coeffs.T, image_low, preferred_element_type=jnp.float32)
        image_back = ((image_dir - image_unit * lax.optimization_barrier(jnp.sum(image_unit * image_dir, axis=-1, keepdims=True))) * image_inv).astype(jnp.bfloat16)
        text_back = (text_dir - text_unit * lax.optimization_barrier(jnp.sum(text_unit * text_dir, axis=-1, keepdims=True))) * text_inv
        weight_total = weight_total + jnp.dot(features.T, image_back, preferred_element_type=jnp.float32)
        losses_all.append(row_sums / BG)
        texts_all.append(text_back)
    return (jnp.stack(losses_all), weight_total / 64.0, jnp.stack(texts_all))
```

```python
import jax
import jax.numpy as jnp
from jax import lax
from jax.experimental import pallas as pl
from jax.experimental.pallas import tpu as pltpu
from jax.sharding import PartitionSpec as P

F32 = jnp.float32
BF16 = jnp.bfloat16
LINE = 4
QUAD = 4
LAYER = 8


def fused_kernel(
    pooled, w_hbm, text_in, pos_in, log_scale, bias,
    loss_out, weight_out, text_out,
    w, text_all, image_all, pos_all, pt_send, pt_all,
    text_unit, image_unit, td_own, td_send, td_recv, id_acc, id_send, id_recv, id_far, id_far_recv,
    loss_part, loss_recv, ib_all, weight_own, wp_send, wp_recv,
    w_sem, tg_s, tg_f, tg_r, ig_s, ig_r, pg_s, pg_r, pt_s, pt_r, td_s, td_r,
    id_s, id_r, ls_s, ls_r, ib_s, ib_f, ib_r, wp_s, wp_r,
):
    blk, x = lax.axis_index("blk"), lax.axis_index("rep")
    z, y, c = blk // 4, (blk // 2) % 2, blk % 2
    rows, emb = text_in.shape
    oy, oc, ox = 1 - y, 1 - c, 1 - x

    def dev(zz, yy, cc, xx):
        return {"blk": zz * 4 + yy * 2 + cc, "rep": xx}

    def layer_of(yy, cc, xx):
        return yy * 4 + cc * 2 + xx

    def layer_dev(j):
        return dev(z, j // 4, (j // 2) % 2, j % 2)

    def remote(src, dst, send, recv, device):
        return pltpu.make_async_remote_copy(
            src_ref=src, dst_ref=dst, send_sem=send, recv_sem=recv,
            device_id=device, device_id_type=pl.DeviceIdType.MESH,
        )

    q, me = y * 2 + c, layer_of(y, c, x)
    far = z // 2
    mid = z * (1 - far) + (LINE - 1 - z) * far

    def flip(base):
        return base + far * (LINE - 1 - 2 * base)

    order = [flip(mid), flip(1 - mid), flip(2), flip(3)]

    w_copy = pltpu.make_async_copy(w_hbm, w, w_sem)
    w_copy.start()
    barrier = pltpu.get_barrier_semaphore()
    for k in range(1, LAYER):
        pl.semaphore_signal(barrier, inc=1, device_id=layer_dev((me + k) % LAYER), device_id_type=pl.DeviceIdType.MESH)
    for k in range(1, LINE):
        pl.semaphore_signal(
            barrier, inc=1, device_id=dev((z + k) % LINE, y, c, x), device_id_type=pl.DeviceIdType.MESH
        )

    raw = text_in[...].astype(F32)
    text_inv = lax.rsqrt(jnp.sum(raw * raw, axis=-1, keepdims=True) + 1e-06)
    unit = raw * text_inv
    text_unit[...] = unit
    text_all[z] = unit.astype(BF16)
    pos_all[q] = pos_in[...]
    pl.semaphore_wait(barrier, LAYER - 1 + LINE - 1)

    own_a = remote(text_all.at[z], text_all.at[z], tg_s.at[0], tg_r.at[z], dev(flip(1 + mid), y, c, x))
    own_b = remote(text_all.at[z], text_all.at[z], tg_s.at[1], tg_r.at[z], dev(flip(0), y, c, x))
    own_a.start()

    @pl.when(mid == 1)
    def _():
        own_b.start()

    peers = [(y, oc), (oy, c), (oy, oc)]
    pos_copies = [
        remote(pos_all.at[q], pos_all.at[q], pg_s.at[k], pg_r.at[q], dev(z, yy, cc, x))
        for k, (yy, cc) in enumerate(peers)
    ]
    for copy in pos_copies:
        copy.start()

    w_copy.wait()
    projected = jnp.dot(pooled[...], w[...], preferred_element_type=F32)
    image_inv = lax.rsqrt(jnp.sum(projected * projected, axis=-1, keepdims=True) + 1e-06)
    unit = projected * image_inv
    image_unit[...] = unit
    image_all[q] = unit.astype(BF16)
    image_copies = [
        remote(image_all.at[q], image_all.at[q], ig_s.at[k], ig_r.at[q], dev(z, yy, cc, x))
        for k, (yy, cc) in enumerate(peers[:2])
    ]
    image_copies[1].start()
    image_copies[0].start()

    turned = pooled[...].T.reshape(LINE, LAYER, -1, rows)
    for j in range(LAYER):
        for t in range(LINE):
            pt_send[j, t] = turned[t, j]
    pt_all[me] = pt_send[me]

    def pt_copy(k):
        j = (me + k) % LAYER
        return remote(pt_send.at[j], pt_all.at[me], pt_s.at[j], pt_r.at[me], layer_dev(j))

    for k in range(1, LAYER):
        pt_copy(k).start()

    def forward(i):
        s = order[i]
        slot = text_all.at[s]
        return remote(slot, slot, tg_f.at[i], tg_r.at[s], dev(flip(2 if i == 1 else 0), y, c, x))

    def arrive(i):
        copy = forward(i)
        copy.wait_recv()

        @pl.when(mid == 1)
        def _():
            copy.start()

    arrive(1)

    @pl.when(mid == 1)
    def _():
        copy = forward(2)
        copy.wait_recv()
        copy.start()

    for k, (yy, cc) in enumerate(peers):
        qq = yy * 2 + cc
        remote(pos_all.at[qq], pos_all.at[qq], pg_s.at[k], pg_r.at[qq], dev(z, yy, cc, x)).wait_recv()

    def image_slot(k, yy, cc):
        slot = image_all.at[yy * 2 + cc]
        return remote(slot, slot, ig_s.at[k], ig_r.at[yy * 2 + cc], dev(z, y, oc, x))

    image_pass = image_slot(2, oy, c)
    image_pass.wait_recv()
    image_pass.start()
    image_slot(0, y, oc).wait_recv()
    image_slot(0, oy, oc).wait_recv()

    images = image_all[...].reshape(QUAD * rows, emb)
    pos = jnp.concatenate([pos_all[k] for k in range(QUAD)], axis=1)
    scale = jnp.exp(jnp.full((1, QUAD * rows), log_scale[0], F32))
    shift = bias[0]
    losses = jnp.zeros((1, QUAD * rows), F32)

    def text_dir_copy(i):
        s = order[i]
        return remote(td_send.at[s], td_recv.at[z], td_s.at[s], td_r.at[z], dev(s, y, c, x))

    for i in range(LINE):
        if i == 2:

            @pl.when(mid == 0)
            def _():
                forward(2).wait_recv()

        if i == 3:
            arrive(3)
        s = order[i]
        text = text_all[s]
        dots = lax.dot_general(text, images, (((1,), (1,)), ((), ())), preferred_element_type=F32)
        logits = scale * dots + shift
        owner = (s * QUAD + q) * rows + lax.broadcasted_iota(jnp.int32, (rows, QUAD * rows), 0)
        sign = jnp.where(owner == pos, 1.0, -1.0).astype(F32)
        value = -sign * logits
        losses += jnp.sum(
            jnp.maximum(value, 0.0) + jnp.log1p(jnp.exp(-jnp.abs(value))), axis=0, keepdims=True
        )
        coeffs = (-sign * jax.nn.sigmoid(value) * scale).astype(BF16)
        text_part = jnp.dot(coeffs, images, preferred_element_type=F32)
        if i == 0:
            td_own[...] = text_part
        else:
            td_send[s] = text_part.astype(BF16)
            text_dir_copy(i).start()
        image_part = lax.dot_general(
            coeffs, text, (((0,), (0,)), ((), ())), preferred_element_type=F32
        ).reshape(QUAD, rows, emb)
        if i == 0:
            id_acc[...] = image_part
        else:
            id_acc[...] += image_part

    id_send[1] = id_acc[oy * 2 + oc].astype(BF16)
    pair = dev(z, y, oc, x)
    id_copies = [remote(id_send.at[k], id_recv.at[k], id_s.at[k], id_r.at[k], pair) for k in range(2)]
    id_copies[1].start()
    id_send[0] = id_acc[y * 2 + oc].astype(BF16)
    id_copies[0].start()
    for k in range(QUAD):
        loss_part[k] = losses[:, k * rows : (k + 1) * rows]
    loss_copies = [
        remote(loss_part.at[yy * 2 + cc], loss_recv.at[q], ls_s.at[k], ls_r.at[q], dev(z, yy, cc, x))
        for k, (yy, cc) in enumerate(peers)
    ]
    for copy in loss_copies:
        copy.start()
    id_copies[1].wait_recv()
    id_far[...] = (id_acc[oy * 2 + c] + id_recv[1].astype(F32)).astype(BF16)
    far_copy = remote(id_far, id_far_recv, id_s.at[2], id_r.at[2], dev(z, oy, c, x))
    far_copy.start()
    id_copies[0].wait_recv()
    near = id_acc[q] + id_recv[0].astype(F32)
    far_copy.wait_recv()
    image_dir = near + id_far_recv[...].astype(F32)
    unit = image_unit[...]
    ib_all[me] = (
        (image_dir - unit * jnp.sum(unit * image_dir, axis=-1, keepdims=True)) * image_inv
    ).astype(BF16)

    others = [(oy, c, ox), (oy, c, x), (y, c, ox), (y, oc, x)]
    ib_copies = [
        remote(ib_all.at[me], ib_all.at[me], ib_s.at[k], ib_r.at[me], dev(z, *other))
        for k, other in enumerate(others)
    ]
    for copy in ib_copies:
        copy.start()

    def ib_slot(k, *other):
        slot = ib_all.at[layer_of(*other)]
        return remote(slot, slot, ib_f.at[k], ib_r.at[layer_of(*other)], pair)

    ib_passes = [ib_slot(k, *other) for k, other in enumerate([(oy, c, x), (y, c, ox), (oy, c, ox)])]
    for copy in ib_passes:
        copy.wait_recv()
        copy.start()
    for other in [(y, oc, x), (oy, oc, x), (y, oc, ox), (oy, oc, ox)]:
        ib_slot(0, *other).wait_recv()

    def pt_recv(k):
        j = (me + k) % LAYER
        return remote(pt_all.at[j], pt_all.at[j], pt_s.at[j], pt_r.at[j], layer_dev(j))

    for k in range(1, LAYER):
        pt_recv(k).wait_recv()

    share = pt_all.shape[2]
    turned_all = jnp.concatenate([pt_all[j].reshape(LINE * share, rows) for j in range(LAYER)], axis=1)
    weight_part = jnp.dot(turned_all, ib_all[...].reshape(LAYER * rows, emb), preferred_element_type=F32)
    for t in range(LINE):
        weight_own[t] = weight_part[t * share : (t + 1) * share]
        wp_send[t] = weight_part[t * share : (t + 1) * share].astype(BF16)

    def weight_copy(k):
        t = (z + k) % LINE
        return remote(wp_send.at[t], wp_recv.at[z], wp_s.at[t], wp_r.at[z], dev(t, y, c, x))

    def from_line(recv, sem, k):
        t = (z + k) % LINE
        return remote(recv.at[t], recv.at[t], wp_s.at[t], sem.at[t], dev(t, y, c, x))

    for k in range(1, LINE):
        weight_copy(k).start()

    total = td_own[...]
    for k in range(1, LINE):
        from_line(td_recv, td_r, k).wait_recv()
        total += td_recv[(z + k) % LINE].astype(F32)
    unit = text_unit[...]
    text_out[...] = (total - unit * jnp.sum(unit * total, axis=-1, keepdims=True)) * text_inv

    total = loss_part[q]
    for k, (yy, cc) in enumerate(peers):
        qq = yy * 2 + cc
        remote(loss_recv.at[qq], loss_recv.at[qq], ls_s.at[k], ls_r.at[qq], dev(z, yy, cc, x)).wait_recv()
        total += loss_recv[qq]
    loss_out[...] = total / (LINE * QUAD * rows)

    total = weight_own[z]
    for k in range(1, LINE):
        from_line(wp_recv, wp_r, k).wait_recv()
        total += wp_recv[(z + k) % LINE].astype(F32)
    weight_out[...] = total / 64.0

    own_a.wait_send()

    @pl.when(mid == 1)
    def _():
        own_b.wait_send()
        for i in range(1, LINE):
            forward(i).wait_send()

    for copy in pos_copies + image_copies + [image_pass] + id_copies + [far_copy] + loss_copies:
        copy.wait_send()
    for copy in ib_copies + ib_passes:
        copy.wait_send()
    for k in range(1, LAYER):
        pt_copy(k).wait_send()
    for k in range(1, LINE):
        text_dir_copy(k).wait_send()
        weight_copy(k).wait_send()


def fused(pooled, w_img, text_emb, pos_index, log_scale, bias):
    _, rows, width = pooled.shape
    emb = w_img.shape[1]
    share = width // (LINE * LAYER)
    vmem, dma = pltpu.VMEM, pltpu.SemaphoreType.DMA
    in_vmem = pl.BlockSpec(memory_space=pltpu.VMEM)
    in_smem = pl.BlockSpec(memory_space=pltpu.SMEM)
    block = (rows, emb)
    loss, weight, text = pl.pallas_call(
        fused_kernel,
        out_shape=(
            jax.ShapeDtypeStruct((1, rows), F32),
            jax.ShapeDtypeStruct((share, emb), F32),
            jax.ShapeDtypeStruct(block, F32),
        ),
        in_specs=[in_vmem, pl.BlockSpec(memory_space=pl.ANY), in_vmem, in_vmem, in_smem, in_smem],
        out_specs=(in_vmem, in_vmem, in_vmem),
        scratch_shapes=[
            vmem((width, emb), BF16),
            vmem((LINE,) + block, BF16),
            vmem((QUAD,) + block, BF16),
            vmem((QUAD, 1, rows), jnp.int32),
            vmem((LAYER, LINE, share, rows), BF16),
            vmem((LAYER, LINE, share, rows), BF16),
            vmem(block, F32),
            vmem(block, F32),
            vmem(block, F32),
            vmem((LINE,) + block, BF16),
            vmem((LINE,) + block, BF16),
            vmem((QUAD,) + block, F32),
            vmem((2,) + block, BF16),
            vmem((2,) + block, BF16),
            vmem(block, BF16),
            vmem(block, BF16),
            vmem((QUAD, 1, rows), F32),
            vmem((QUAD, 1, rows), F32),
            vmem((LAYER,) + block, BF16),
            vmem((LINE, share, emb), F32),
            vmem((LINE, share, emb), BF16),
            vmem((LINE, share, emb), BF16),
            dma,
            dma((2,)), dma((LINE,)), dma((LINE,)),
            dma((3,)), dma((QUAD,)),
            dma((3,)), dma((QUAD,)),
            dma((LAYER,)), dma((LAYER,)),
            dma((LINE,)), dma((LINE,)),
            dma((3,)), dma((3,)),
            dma((3,)), dma((QUAD,)),
            dma((4,)), dma((3,)), dma((LAYER,)),
            dma((LINE,)), dma((LINE,)),
        ],
        compiler_params=pltpu.CompilerParams(
            collective_id=0, has_side_effects=True, vmem_limit_bytes=48 * 2**20
        ),
    )(pooled[0], w_img, text_emb[0], pos_index, log_scale, bias)
    return loss, weight, text[None]


def normalize(rows):
    squares = jnp.sum(rows * rows, axis=-1, keepdims=True)
    inverse = lax.rsqrt(squares + 1e-06)
    return (rows * inverse, inverse)


def pair_terms(left, right, left_pos, right_start, scale_value, shift):
    logits = scale_value * jnp.dot(left, right.T, preferred_element_type=jnp.float32) + shift
    columns = right_start + jnp.arange(right.shape[0], dtype=jnp.int32)
    sign = jnp.where(left_pos[:, None] == columns[None, :], 1.0, -1.0).astype(jnp.float32)
    losses = jax.nn.softplus(-sign * logits)
    coeffs = (-sign * jax.nn.sigmoid(-sign * logits) * scale_value).astype(jnp.bfloat16)
    return (jnp.sum(losses, axis=1), coeffs)


def transpose_dot(coeffs, rows):
    return lax.dot_general(
        coeffs, rows, (((0,), (0,)), ((), ())), preferred_element_type=jnp.float32
    )


def plain(pooled, w_img, text_emb, pos_index, log_scale, bias):
    scale_value = jnp.exp(log_scale[0])
    shift = bias[0]
    features = pooled[0]
    my_pos = pos_index[0]
    row_count = features.shape[0]
    group_size = row_count * lax.axis_size("blk")
    my_start = lax.axis_index("blk") * row_count
    projected = jnp.dot(features, w_img, preferred_element_type=jnp.float32)
    image_unit, image_inv = normalize(projected)
    image_low = image_unit.astype(jnp.bfloat16)
    text_unit, text_inv = normalize(text_emb[0].astype(jnp.float32))
    text_low = text_unit.astype(jnp.bfloat16)
    piece = lax.all_gather(text_low, "blk", axis=0, tiled=True)
    row_sums, coeffs = pair_terms(image_low, piece, my_pos, jnp.int32(0), scale_value, shift)
    loss_total = row_sums
    image_dir = jnp.dot(coeffs, piece, preferred_element_type=jnp.float32)
    pieces = (
        lax.all_gather(image_low, "blk", axis=0, tiled=True),
        lax.all_gather(my_pos, "blk", axis=0, tiled=True),
    )
    row_sums, coeffs = pair_terms(pieces[0], text_low, pieces[1], my_start, scale_value, shift)
    text_dir = transpose_dot(coeffs, pieces[0])
    image_back = (
        (image_dir - image_unit * jnp.sum(image_unit * image_dir, axis=-1, keepdims=True))
        * image_inv
    ).astype(jnp.bfloat16)
    text_back = (
        text_dir - text_unit * jnp.sum(text_unit * text_dir, axis=-1, keepdims=True)
    ) * text_inv
    weight_part = transpose_dot(features, image_back)
    weight_sum = lax.psum_scatter(weight_part, ("blk", "rep"), scatter_dimension=0, tiled=True)
    return ((loss_total / group_size)[None], weight_sum / 64.0, text_back[None])


def solution(mesh):
    def shards(pooled, w_img, text_emb, pos_index, log_scale, bias):
        _, rows, width = pooled.shape
        fits = mesh.shape["blk"] == LINE * QUAD and mesh.shape["rep"] * QUAD == LAYER
        fits = fits and rows % 128 == 0 and width % (LINE * LAYER * 16) == 0
        return (fused if fits else plain)(pooled, w_img, text_emb, pos_index, log_scale, bias)

    return jax.shard_map(
        shards,
        mesh=mesh,
        in_specs=(P("rep", "blk", None), P(), P("rep", "blk", None), P("rep", "blk"), P(), P()),
        out_specs=(P("rep", "blk"), P(("blk", "rep"), None), P("rep", "blk", None)),
        check_vma=False,
    )
```

```python
import jax
import jax.numpy as jnp
from jax import lax
from jax.experimental import pallas as pl
from jax.experimental.pallas import tpu as pltpu
from jax.sharding import PartitionSpec as P

F32 = jnp.float32
BF16 = jnp.bfloat16
LINE = 4
QUAD = 4
LAYER = 8
PARTS = 4


def fused_kernel(
    pooled_hbm, w_hbm, text_hbm, pos_hbm, log_scale, bias,
    loss_out, weight_out, text_out,
    pooled, w, text_in, pos_in, text_all, image_all, pos_all, pt_send, pt_all,
    text_unit, image_unit, td_own, td_send, td_recv, id_acc, id_send, id_recv, id_far, id_far_recv,
    coeff_parts, loss_part, loss_recv, ib_all, weight_own, wp_send, wp_recv,
    in_sem, tg_s, tg_f, tg_r, ig_s, ig_r, pg_s, pg_r, pt_s, pt_r, td_s, td_r,
    id_s, id_r, ls_s, ls_r, ib_s, ib_f, ib_d, ib_r, wp_s, wp_r,
):
    blk, x = lax.axis_index("blk"), lax.axis_index("rep")
    z, y, c = blk // 4, (blk // 2) % 2, blk % 2
    rows, emb = text_in.shape
    oy, oc, ox = 1 - y, 1 - c, 1 - x

    def dev(zz, yy, cc, xx):
        return {"blk": zz * 4 + yy * 2 + cc, "rep": xx}

    def layer_of(yy, cc, xx):
        return yy * 4 + cc * 2 + xx

    def layer_dev(j):
        return dev(z, j // 4, (j // 2) % 2, j % 2)

    def remote(src, dst, send, recv, device):
        return pltpu.make_async_remote_copy(
            src_ref=src, dst_ref=dst, send_sem=send, recv_sem=recv,
            device_id=device, device_id_type=pl.DeviceIdType.MESH,
        )

    q, me = y * 2 + c, layer_of(y, c, x)
    far = z // 2
    mid = z * (1 - far) + (LINE - 1 - z) * far

    def flip(base):
        return base + far * (LINE - 1 - 2 * base)

    order = [flip(mid), flip(1 - mid), flip(2), flip(3)]

    ins = [(text_hbm, text_in), (pos_hbm, pos_in), (pooled_hbm, pooled), (w_hbm, w)]
    ins = [pltpu.make_async_copy(src, dst, in_sem.at[k]) for k, (src, dst) in enumerate(ins)]
    for copy in ins:
        copy.start()
    barrier = pltpu.get_barrier_semaphore()
    for k in range(1, LAYER):
        pl.semaphore_signal(barrier, inc=1, device_id=layer_dev((me + k) % LAYER), device_id_type=pl.DeviceIdType.MESH)
    for k in range(1, LINE):
        pl.semaphore_signal(
            barrier, inc=1, device_id=dev((z + k) % LINE, y, c, x), device_id_type=pl.DeviceIdType.MESH
        )

    ins[0].wait()
    raw = text_in[...].astype(F32)
    text_inv = lax.rsqrt(jnp.sum(raw * raw, axis=-1, keepdims=True) + 1e-06)
    unit = raw * text_inv
    text_unit[...] = unit
    text_all[z] = unit.astype(BF16)
    ins[1].wait()
    pos_all[q] = pos_in[...]
    pl.semaphore_wait(barrier, LAYER - 1 + LINE - 1)

    own_a = remote(text_all.at[z], text_all.at[z], tg_s.at[0], tg_r.at[z], dev(flip(1 + mid), y, c, x))
    own_b = remote(text_all.at[z], text_all.at[z], tg_s.at[1], tg_r.at[z], dev(flip(0), y, c, x))
    own_a.start()

    @pl.when(mid == 1)
    def _():
        own_b.start()

    peers = [(y, oc), (oy, c), (oy, oc)]
    pos_copies = [
        remote(pos_all.at[q], pos_all.at[q], pg_s.at[k], pg_r.at[q], dev(z, yy, cc, x))
        for k, (yy, cc) in enumerate(peers)
    ]
    for copy in pos_copies:
        copy.start()

    ins[2].wait()
    ins[3].wait()
    projected = jnp.dot(pooled[...], w[...], preferred_element_type=F32)
    image_inv = lax.rsqrt(jnp.sum(projected * projected, axis=-1, keepdims=True) + 1e-06)
    unit = projected * image_inv
    image_unit[...] = unit
    image_all[q] = unit.astype(BF16)
    image_copies = [
        remote(image_all.at[q], image_all.at[q], ig_s.at[k], ig_r.at[q], dev(z, yy, cc, x))
        for k, (yy, cc) in enumerate(peers[:2])
    ]
    image_copies[1].start()
    image_copies[0].start()

    turned = pooled[...].T.reshape(LINE, LAYER, -1, rows)
    for j in range(LAYER):
        for t in range(LINE):
            pt_send[j, t] = turned[t, j]
    pt_all[me] = pt_send[me]

    def pt_copy(k):
        j = (me + k) % LAYER
        return remote(pt_send.at[j], pt_all.at[me], pt_s.at[j], pt_r.at[me], layer_dev(j))

    def forward(i):
        s = order[i]
        slot = text_all.at[s]
        return remote(slot, slot, tg_f.at[i], tg_r.at[s], dev(flip(2 if i == 1 else 0), y, c, x))

    def arrive(i):
        copy = forward(i)
        copy.wait_recv()

        @pl.when(mid == 1)
        def _():
            copy.start()

    arrive(1)

    @pl.when(mid == 1)
    def _():
        copy = forward(2)
        copy.wait_recv()
        copy.start()

    for k, (yy, cc) in enumerate(peers):
        qq = yy * 2 + cc
        remote(pos_all.at[qq], pos_all.at[qq], pg_s.at[k], pg_r.at[qq], dev(z, yy, cc, x)).wait_recv()

    def image_slot(k, yy, cc):
        slot = image_all.at[yy * 2 + cc]
        return remote(slot, slot, ig_s.at[k], ig_r.at[yy * 2 + cc], dev(z, y, oc, x))

    image_pass = image_slot(2, oy, c)
    image_pass.wait_recv()
    image_pass.start()
    image_slot(0, y, oc).wait_recv()
    image_slot(0, oy, oc).wait_recv()

    for k in range(1, LAYER):
        pt_copy(k).start()

    images = image_all[...].reshape(QUAD * rows, emb)
    pos = jnp.concatenate([pos_all[k] for k in range(QUAD)], axis=1)
    scale = jnp.exp(jnp.full((1, QUAD * rows), log_scale[0], F32))
    shift = bias[0]
    losses = jnp.zeros((1, QUAD * rows), F32)

    def text_dir_copy(i):
        s = order[i]
        return remote(td_send.at[s], td_recv.at[z], td_s.at[s], td_r.at[z], dev(s, y, c, x))

    for i in range(LINE):
        if i == 2:

            @pl.when(mid == 0)
            def _():
                forward(2).wait_recv()

        if i == 3:
            arrive(3)
        s = order[i]
        text = text_all[s]
        dots = lax.dot_general(text, images, (((1,), (1,)), ((), ())), preferred_element_type=F32)
        logits = scale * dots + shift
        owner = (s * QUAD + q) * rows + lax.broadcasted_iota(jnp.int32, (rows, QUAD * rows), 0)
        sign = jnp.where(owner == pos, 1.0, -1.0).astype(F32)
        value = -sign * logits
        losses += jnp.sum(
            jnp.maximum(value, 0.0) + jnp.log1p(jnp.exp(-jnp.abs(value))), axis=0, keepdims=True
        )
        coeffs = (-sign * jax.nn.sigmoid(value) * scale).astype(BF16)
        if i == LINE - 1:
            break
        text_part = jnp.dot(coeffs, images, preferred_element_type=F32)
        if i == 0:
            td_own[...] = text_part
        else:
            td_send[s] = text_part.astype(BF16)
        if i == 1:

            @pl.when(mid == 0)
            def _():
                text_dir_copy(1).start()

        if i == 2:
            text_dir_copy(2).start()
        image_part = lax.dot_general(
            coeffs, text, (((0,), (0,)), ((), ())), preferred_element_type=F32
        ).reshape(QUAD, rows, emb)
        if i == 0:
            id_acc[...] = image_part
        else:
            id_acc[...] += image_part

    for k in range(QUAD):
        coeff_parts[k] = coeffs[:, k * rows : (k + 1) * rows]
        loss_part[k] = losses[:, k * rows : (k + 1) * rows]

    def image_sum(yy, cc):
        return id_acc[yy * 2 + cc] + lax.dot_general(
            coeff_parts[yy * 2 + cc], text, (((0,), (0,)), ((), ())), preferred_element_type=F32
        )

    pair = dev(z, y, oc, x)
    id_copies = [remote(id_send.at[k], id_recv.at[k], id_s.at[k], id_r.at[k], pair) for k in range(2)]
    id_send[1] = image_sum(oy, oc).astype(BF16)
    id_copies[1].start()
    id_send[0] = image_sum(y, oc).astype(BF16)
    id_copies[0].start()
    id_acc[oy * 2 + c] = image_sum(oy, c)
    id_copies[1].wait_recv()
    id_far[...] = (id_acc[oy * 2 + c] + id_recv[1].astype(F32)).astype(BF16)
    far_copy = remote(id_far, id_far_recv, id_s.at[2], id_r.at[2], dev(z, oy, c, x))
    far_copy.start()
    near = image_sum(y, c)
    td_send[s] = jnp.dot(coeffs, images, preferred_element_type=F32).astype(BF16)

    @pl.when(mid == 1)
    def _():
        text_dir_copy(1).start()

    text_dir_copy(3).start()
    loss_copies = [
        remote(loss_part.at[yy * 2 + cc], loss_recv.at[q], ls_s.at[k], ls_r.at[q], dev(z, yy, cc, x))
        for k, (yy, cc) in enumerate(peers)
    ]
    for copy in loss_copies:
        copy.start()
    id_copies[0].wait_recv()
    near += id_recv[0].astype(F32)
    far_copy.wait_recv()
    image_dir = near + id_far_recv[...].astype(F32)
    unit = image_unit[...]
    image_back = (
        (image_dir - unit * jnp.sum(unit * image_dir, axis=-1, keepdims=True)) * image_inv
    ).astype(BF16)
    part = emb // PARTS
    for k in range(PARTS):
        ib_all[k, me] = image_back[:, k * part : (k + 1) * part]

    def ib_copy(k, slot, send, *to):
        j = layer_of(*slot)
        return remote(ib_all.at[k, j], ib_all.at[k, j], send, ib_r.at[k, j], dev(z, *to))

    own, pair, by_y, by_x, diagonal = (y, c, x), (y, oc, x), (oy, c, x), (y, c, ox), (oy, c, ox)
    ib_copies = [
        ib_copy(k, own, ib_s.at[k, n], *to) for k in range(PARTS) for n, to in enumerate((by_x, by_y, pair))
    ]
    for copy in ib_copies:
        copy.start()

    def pt_recv(k):
        j = (me + k) % LAYER
        return remote(pt_all.at[j], pt_all.at[j], pt_s.at[j], pt_r.at[j], layer_dev(j))

    for k in range(1, LAYER):
        pt_recv(k).wait_recv()

    share = pt_all.shape[2]
    turned_all = jnp.concatenate([pt_all[j].reshape(LINE * share, rows) for j in range(LAYER)], axis=1)

    def weight_copy(k, n):
        t = (z + n) % LINE
        return remote(wp_send.at[k, t], wp_recv.at[k, z], wp_s.at[k, t], wp_r.at[k, z], dev(t, y, c, x))

    for step in range(PARTS + 2):
        k = step
        if k < PARTS:
            for n, slot in enumerate((by_x, by_y)):
                ib_copy(k, slot, ib_f.at[k, n], *pair).wait_recv()
                if k % 2 == n:
                    on = ib_copy(k, slot, ib_d.at[k], *(by_y if n == 0 else by_x))
                    on.start()
                    ib_copies.append(on)
                on = ib_copy(k, slot, ib_f.at[k, n], *pair)
                on.start()
                ib_copies.append(on)
        k = step - 1
        if 0 <= k < PARTS:
            on = ib_copy(k, diagonal, ib_f.at[k, 2], *pair)
            on.wait_recv()
            on.start()
            ib_copies.append(on)
        k = step - 2
        if k < 0:
            continue
        for slot in ((y, oc, x), (oy, oc, x), (y, oc, ox), (oy, oc, ox)):
            ib_copy(k, slot, ib_f.at[k, 0], *pair).wait_recv()
        product = jnp.dot(turned_all, ib_all[k].reshape(LAYER * rows, part), preferred_element_type=F32)
        for t in range(LINE):
            weight_own[k, t] = product[t * share : (t + 1) * share]
            wp_send[k, t] = product[t * share : (t + 1) * share].astype(BF16)
        for n in range(1, LINE):
            weight_copy(k, n).start()

    total = td_own[...]
    for k in range(1, LINE):
        t = (z + k) % LINE
        remote(td_recv.at[t], td_recv.at[t], td_s.at[t], td_r.at[t], dev(t, y, c, x)).wait_recv()
        total += td_recv[t].astype(F32)
    unit = text_unit[...]
    text_out[...] = (total - unit * jnp.sum(unit * total, axis=-1, keepdims=True)) * text_inv

    total = loss_part[q]
    for k, (yy, cc) in enumerate(peers):
        qq = yy * 2 + cc
        remote(loss_recv.at[qq], loss_recv.at[qq], ls_s.at[k], ls_r.at[qq], dev(z, yy, cc, x)).wait_recv()
        total += loss_recv[qq]
    loss_out[...] = total / (LINE * QUAD * rows)

    for k in range(PARTS):
        total = weight_own[k, z]
        for n in range(1, LINE):
            t = (z + n) % LINE
            slot = wp_recv.at[k, t]
            remote(slot, slot, wp_s.at[k, t], wp_r.at[k, t], dev(t, y, c, x)).wait_recv()
            total += wp_recv[k, t].astype(F32)
        weight_out[:, k * part : (k + 1) * part] = total / 64.0

    own_a.wait_send()

    @pl.when(mid == 1)
    def _():
        own_b.wait_send()
        for i in range(1, LINE):
            forward(i).wait_send()

    for copy in pos_copies + image_copies + [image_pass] + id_copies + [far_copy] + loss_copies:
        copy.wait_send()
    for copy in ib_copies:
        copy.wait_send()
    for k in range(1, LAYER):
        pt_copy(k).wait_send()
    for k in range(1, LINE):
        text_dir_copy(k).wait_send()
        for part in range(PARTS):
            weight_copy(part, k).wait_send()


def fused(pooled, w_img, text_emb, pos_index, log_scale, bias):
    _, rows, width = pooled.shape
    emb = w_img.shape[1]
    share = width // (LINE * LAYER)
    vmem, dma = pltpu.VMEM, pltpu.SemaphoreType.DMA
    in_vmem = pl.BlockSpec(memory_space=pltpu.VMEM)
    in_hbm = pl.BlockSpec(memory_space=pltpu.HBM)
    in_smem = pl.BlockSpec(memory_space=pltpu.SMEM)
    block = (rows, emb)
    loss, weight, text = pl.pallas_call(
        fused_kernel,
        out_shape=(
            jax.ShapeDtypeStruct((1, rows), F32),
            jax.ShapeDtypeStruct((share, emb), F32),
            jax.ShapeDtypeStruct(block, F32),
        ),
        in_specs=[in_hbm, in_hbm, in_hbm, in_hbm, in_smem, in_smem],
        out_specs=(in_vmem, in_vmem, in_vmem),
        scratch_shapes=[
            vmem((rows, width), BF16),
            vmem((width, emb), BF16),
            vmem(block, BF16),
            vmem((1, rows), jnp.int32),
            vmem((LINE,) + block, BF16),
            vmem((QUAD,) + block, BF16),
            vmem((QUAD, 1, rows), jnp.int32),
            vmem((LAYER, LINE, share, rows), BF16),
            vmem((LAYER, LINE, share, rows), BF16),
            vmem(block, F32),
            vmem(block, F32),
            vmem(block, F32),
            vmem((LINE,) + block, BF16),
            vmem((LINE,) + block, BF16),
            vmem((QUAD,) + block, F32),
            vmem((2,) + block, BF16),
            vmem((2,) + block, BF16),
            vmem(block, BF16),
            vmem(block, BF16),
            vmem((QUAD, rows, rows), BF16),
            vmem((QUAD, 1, rows), F32),
            vmem((QUAD, 1, rows), F32),
            vmem((PARTS, LAYER, rows, emb // PARTS), BF16),
            vmem((PARTS, LINE, share, emb // PARTS), F32),
            vmem((PARTS, LINE, share, emb // PARTS), BF16),
            vmem((PARTS, LINE, share, emb // PARTS), BF16),
            dma((4,)),
            dma((2,)), dma((LINE,)), dma((LINE,)),
            dma((3,)), dma((QUAD,)),
            dma((3,)), dma((QUAD,)),
            dma((LAYER,)), dma((LAYER,)),
            dma((LINE,)), dma((LINE,)),
            dma((3,)), dma((3,)),
            dma((3,)), dma((QUAD,)),
            dma((PARTS, 3)), dma((PARTS, 3)), dma((PARTS,)), dma((PARTS, LAYER)),
            dma((PARTS, LINE)), dma((PARTS, LINE)),
        ],
        compiler_params=pltpu.CompilerParams(
            collective_id=0, has_side_effects=True, vmem_limit_bytes=63 * 2**20
        ),
    )(pooled[0], w_img, text_emb[0], pos_index, log_scale, bias)
    return loss, weight, text[None]


def normalize(rows):
    squares = jnp.sum(rows * rows, axis=-1, keepdims=True)
    inverse = lax.rsqrt(squares + 1e-06)
    return (rows * inverse, inverse)


def pair_terms(left, right, left_pos, right_start, scale_value, shift):
    logits = scale_value * jnp.dot(left, right.T, preferred_element_type=jnp.float32) + shift
    columns = right_start + jnp.arange(right.shape[0], dtype=jnp.int32)
    sign = jnp.where(left_pos[:, None] == columns[None, :], 1.0, -1.0).astype(jnp.float32)
    losses = jax.nn.softplus(-sign * logits)
    coeffs = (-sign * jax.nn.sigmoid(-sign * logits) * scale_value).astype(jnp.bfloat16)
    return (jnp.sum(losses, axis=1), coeffs)


def transpose_dot(coeffs, rows):
    return lax.dot_general(
        coeffs, rows, (((0,), (0,)), ((), ())), preferred_element_type=jnp.float32
    )


def plain(pooled, w_img, text_emb, pos_index, log_scale, bias):
    scale_value = jnp.exp(log_scale[0])
    shift = bias[0]
    features = pooled[0]
    my_pos = pos_index[0]
    row_count = features.shape[0]
    group_size = row_count * lax.axis_size("blk")
    my_start = lax.axis_index("blk") * row_count
    projected = jnp.dot(features, w_img, preferred_element_type=jnp.float32)
    image_unit, image_inv = normalize(projected)
    image_low = image_unit.astype(jnp.bfloat16)
    text_unit, text_inv = normalize(text_emb[0].astype(jnp.float32))
    text_low = text_unit.astype(jnp.bfloat16)
    piece = lax.all_gather(text_low, "blk", axis=0, tiled=True)
    row_sums, coeffs = pair_terms(image_low, piece, my_pos, jnp.int32(0), scale_value, shift)
    loss_total = row_sums
    image_dir = jnp.dot(coeffs, piece, preferred_element_type=jnp.float32)
    pieces = (
        lax.all_gather(image_low, "blk", axis=0, tiled=True),
        lax.all_gather(my_pos, "blk", axis=0, tiled=True),
    )
    row_sums, coeffs = pair_terms(pieces[0], text_low, pieces[1], my_start, scale_value, shift)
    text_dir = transpose_dot(coeffs, pieces[0])
    image_back = (
        (image_dir - image_unit * jnp.sum(image_unit * image_dir, axis=-1, keepdims=True))
        * image_inv
    ).astype(jnp.bfloat16)
    text_back = (
        text_dir - text_unit * jnp.sum(text_unit * text_dir, axis=-1, keepdims=True)
    ) * text_inv
    weight_part = transpose_dot(features, image_back)
    weight_sum = lax.psum_scatter(weight_part, ("blk", "rep"), scatter_dimension=0, tiled=True)
    return ((loss_total / group_size)[None], weight_sum / 64.0, text_back[None])


def solution(mesh):
    def shards(pooled, w_img, text_emb, pos_index, log_scale, bias):
        _, rows, width = pooled.shape
        fits = mesh.shape["blk"] == LINE * QUAD and mesh.shape["rep"] * QUAD == LAYER
        fits = fits and rows % 128 == 0 and width % (LINE * LAYER * 16) == 0
        return (fused if fits else plain)(pooled, w_img, text_emb, pos_index, log_scale, bias)

    return jax.shard_map(
        shards,
        mesh=mesh,
        in_specs=(P("rep", "blk", None), P(), P("rep", "blk", None), P("rep", "blk"), P(), P()),
        out_specs=(P("rep", "blk"), P(("blk", "rep"), None), P("rep", "blk", None)),
        check_vma=False,
    )
```

```python
import jax
import jax.numpy as jnp
from jax import lax
from jax.experimental import pallas as pl
from jax.experimental.pallas import tpu as pltpu
from jax.sharding import PartitionSpec as P

F32 = jnp.float32
BF16 = jnp.bfloat16
LINE = 4
QUAD = 4
LAYER = 8
PIECES = 4
PARTS = 4


def fused_kernel(
    pooled_hbm, w_hbm, text_hbm, pos_hbm, log_scale, bias,
    loss_out, weight_out, text_out,
    pooled, w, text_in, pos_in, text_all, image_all, pos_all, pt_send, pt_all,
    text_unit, image_unit, td_acc, td_send, td_recv, id_acc, id_send, id_recv, id_far, id_far_recv,
    coeff_parts, loss_part, loss_recv, ib_all, weight_own, wp_send, wp_recv,
    in_sem, tg_s, tg_f, tg_y, tg_r, ig_s, ig_r, pg_s, pg_r, pt_s, pt_r, td_s, td_r,
    id_s, id_r, ls_s, ls_r, ib_s, ib_f, ib_d, ib_r, wp_s, wp_r,
):
    blk, x = lax.axis_index("blk"), lax.axis_index("rep")
    z, y, c = blk // 4, (blk // 2) % 2, blk % 2
    rows, emb = text_in.shape
    oy, oc, ox = 1 - y, 1 - c, 1 - x

    def dev(zz, yy, cc, xx):
        return {"blk": zz * 4 + yy * 2 + cc, "rep": xx}

    def layer_of(yy, cc, xx):
        return yy * 4 + cc * 2 + xx

    def layer_dev(j):
        return dev(z, j // 4, (j // 2) % 2, j % 2)

    def remote(src, dst, send, recv, device):
        return pltpu.make_async_remote_copy(
            src_ref=src, dst_ref=dst, send_sem=send, recv_sem=recv,
            device_id=device, device_id_type=pl.DeviceIdType.MESH,
        )

    half, odd = z // 2, z % 2
    other_half, other_odd = 1 - half, 1 - odd
    z_far, z_near = other_half * 2 + odd, half * 2 + other_odd
    me = layer_of(y, c, x)

    ins = [(text_hbm, text_in), (pos_hbm, pos_in), (pooled_hbm, pooled), (w_hbm, w)]
    ins = [pltpu.make_async_copy(src, dst, in_sem.at[k]) for k, (src, dst) in enumerate(ins)]
    for copy in ins:
        copy.start()
    barrier = pltpu.get_barrier_semaphore()
    for k in range(1, LAYER):
        pl.semaphore_signal(barrier, inc=1, device_id=layer_dev((me + k) % LAYER), device_id_type=pl.DeviceIdType.MESH)
    for k in range(1, LINE):
        pl.semaphore_signal(
            barrier, inc=1, device_id=dev((z + k) % LINE, y, c, x), device_id_type=pl.DeviceIdType.MESH
        )
    pl.semaphore_signal(barrier, inc=1, device_id=dev(z_near, y, oc, x), device_id_type=pl.DeviceIdType.MESH)

    ins[0].wait()
    raw = text_in[...].astype(F32)
    text_inv = lax.rsqrt(jnp.sum(raw * raw, axis=-1, keepdims=True) + 1e-06)
    unit = raw * text_inv
    text_unit[...] = unit
    text_all[half, y] = unit.astype(BF16)
    ins[1].wait()
    pos_all[odd, c] = pos_in[...]
    pl.semaphore_wait(barrier, LAYER - 1 + LINE)

    piece = rows // PIECES

    def text_piece(hh, yy, k, send, *to):
        slot = text_all.at[hh, yy, pl.ds(k * piece, piece)]
        return remote(slot, slot, send, tg_r.at[hh, yy, k], dev(*to))

    far_texts = [text_piece(half, y, k, tg_s.at[k], z_far, y, c, x) for k in range(PIECES)]
    for copy in far_texts:
        copy.start()

    def text_whole(yy):
        slot = text_all.at[half, yy]
        return remote(slot, slot, tg_y, tg_r.at[half, yy, 0], dev(z, oy, c, x))

    text_whole(y).start()

    peers = [(odd, oc), (other_odd, c), (other_odd, oc)]

    def peer_dev(oo, cc):
        return dev(half * 2 + oo, y, cc, x)

    pos_copies = [
        remote(pos_all.at[odd, c], pos_all.at[odd, c], pg_s.at[k], pg_r.at[odd, c], peer_dev(*peer))
        for k, peer in enumerate(peers)
    ]
    for copy in pos_copies:
        copy.start()

    ins[2].wait()
    ins[3].wait()
    projected = jnp.dot(pooled[...], w[...], preferred_element_type=F32)
    image_inv = lax.rsqrt(jnp.sum(projected * projected, axis=-1, keepdims=True) + 1e-06)
    unit = projected * image_inv
    image_unit[...] = unit
    image_all[odd, c] = unit.astype(BF16)

    def image_copy(k, oo, cc, to):
        slot = image_all.at[oo, cc]
        return remote(slot, slot, ig_s.at[k], ig_r.at[oo, cc], peer_dev(*to))

    image_copies = [image_copy(k, odd, c, to) for k, to in enumerate(peers[:2])]
    image_copies[1].start()
    image_copies[0].start()

    turned = pooled[...].T.reshape(LINE, LAYER, -1, rows)
    for j in range(LAYER):
        for t in range(LINE):
            pt_send[j, t] = turned[t, j]
    pt_all[me] = pt_send[me]

    def pt_copy(k):
        j = (me + k) % LAYER
        return remote(pt_send.at[j], pt_all.at[me], pt_s.at[j], pt_r.at[me], layer_dev(j))

    scale = jnp.exp(jnp.full((1, 2 * rows), log_scale[0], F32))
    shift = bias[0]

    def pairs(owners, oo):
        text = jnp.concatenate([text_all[hh, yy] for hh, yy in owners], axis=0)
        images = image_all[oo].reshape(2 * rows, emb)
        pos = jnp.concatenate([pos_all[oo, 0], pos_all[oo, 1]], axis=1)
        dots = lax.dot_general(text, images, (((1,), (1,)), ((), ())), preferred_element_type=F32)
        logits = scale * dots + shift
        index = lax.broadcasted_iota(jnp.int32, (rows, 2 * rows), 0)
        index = jnp.concatenate([((hh * 2 + odd) * 4 + yy * 2 + c) * rows + index for hh, yy in owners], axis=0)
        sign = jnp.where(index == pos, 1.0, -1.0).astype(F32)
        value = -sign * logits
        losses = jnp.sum(
            jnp.maximum(value, 0.0) + jnp.log1p(jnp.exp(-jnp.abs(value))), axis=0, keepdims=True
        )
        coeffs = (-sign * jax.nn.sigmoid(value) * scale).astype(BF16)
        return text, images, coeffs, losses

    def text_terms(coeffs, images):
        return jnp.dot(coeffs, images, preferred_element_type=F32)

    def image_terms(coeffs, text):
        return lax.dot_general(coeffs, text, (((0,), (0,)), ((), ())), preferred_element_type=F32)

    here, by_y, ahead, across = (half, y), (half, oy), (other_half, y), (other_half, oy)

    for k, peer in enumerate(peers):
        remote(pos_all.at[peer], pos_all.at[peer], pg_s.at[k], pg_r.at[peer], peer_dev(*peer)).wait_recv()
    text_whole(oy).wait_recv()
    image_copy(0, odd, oc, peers[0]).wait_recv()
    text, images, coeffs, loss_here = pairs([here, by_y], odd)
    terms = text_terms(coeffs, images)
    td_acc[here] = terms[:rows]
    td_acc[by_y] = terms[rows:]
    id_acc[odd] = image_terms(coeffs, text).reshape(2, rows, emb)

    text_passes = []
    for k in range(PIECES):
        copy = text_piece(*ahead, k, tg_f.at[k], z, oy, c, x)
        copy.wait_recv()
        copy.start()
        text_passes.append(copy)
    text, images, coeffs, losses = pairs([ahead], odd)
    loss_here += losses
    td_acc[ahead] = text_terms(coeffs, images)
    id_acc[odd] += image_terms(coeffs, text).reshape(2, rows, emb)

    image_pass = image_copy(2, other_odd, c, peers[0])
    image_pass.wait_recv()
    image_pass.start()
    for k in range(1, LAYER):
        pt_copy(k).start()
    image_copy(0, other_odd, oc, peers[0]).wait_recv()
    text, images, coeffs, loss_near = pairs([here, by_y, ahead], other_odd)
    terms = text_terms(coeffs, images)
    td_send[0] = (td_acc[by_y] + terms[rows : 2 * rows]).astype(BF16)

    def td_copy(k, *to):
        return remote(td_send.at[k], td_recv.at[k], td_s.at[k], td_r.at[k], dev(*to))

    td_copies = [td_copy(0, z, oy, c, x), td_copy(1, z, oy, c, x), td_copy(2, z_far, y, c, x)]
    td_copies[0].start()
    td_acc[here] += terms[:rows]
    td_acc[ahead] += terms[2 * rows :]
    id_acc[other_odd] = image_terms(coeffs, text).reshape(2, rows, emb)

    for k in range(PIECES):
        text_piece(*across, k, tg_f.at[k], z, oy, c, x).wait_recv()

    def image_sum(oo, cc):
        return id_acc[oo, cc] + image_terms(coeff_parts[oo, cc], text)

    pair = dev(z, y, oc, x)
    id_copies = [remote(id_send.at[k], id_recv.at[k], id_s.at[k], id_r.at[k], pair) for k in range(2)]
    text, images, coeffs, losses = pairs([across], other_odd)
    loss_near += losses
    for k in range(2):
        coeff_parts[other_odd, k] = coeffs[:, k * rows : (k + 1) * rows]
    id_send[1] = image_sum(other_odd, oc).astype(BF16)
    id_copies[1].start()
    id_acc[other_odd, c] = image_sum(other_odd, c)
    near_images, near_coeffs = images, coeffs
    text, images, coeffs, losses = pairs([across], odd)
    loss_here += losses
    for k in range(2):
        coeff_parts[odd, k] = coeffs[:, k * rows : (k + 1) * rows]
    id_send[0] = image_sum(odd, oc).astype(BF16)
    id_copies[0].start()
    for k in range(2):
        loss_part[odd, k] = loss_here[:, k * rows : (k + 1) * rows]
        loss_part[other_odd, k] = loss_near[:, k * rows : (k + 1) * rows]
    id_copies[1].wait_recv()
    id_far[...] = (id_acc[other_odd, c] + id_recv[1].astype(F32)).astype(BF16)
    far_copy = remote(id_far, id_far_recv, id_s.at[2], id_r.at[2], dev(z_near, y, c, x))
    far_copy.start()
    td_send[1] = (text_terms(coeffs, images) + text_terms(near_coeffs, near_images)).astype(BF16)
    td_copies[1].start()
    near = image_sum(odd, c)
    loss_copies = [
        remote(loss_part.at[peer], loss_recv.at[odd, c], ls_s.at[k], ls_r.at[odd, c], peer_dev(*peer))
        for k, peer in enumerate(peers)
    ]
    for copy in loss_copies:
        copy.start()
    id_copies[0].wait_recv()
    near += id_recv[0].astype(F32)
    far_copy.wait_recv()
    image_dir = near + id_far_recv[...].astype(F32)
    unit = image_unit[...]
    image_back = (
        (image_dir - unit * jnp.sum(unit * image_dir, axis=-1, keepdims=True)) * image_inv
    ).astype(BF16)
    part = emb // PARTS
    for k in range(PARTS):
        ib_all[k, me] = image_back[:, k * part : (k + 1) * part]

    def ib_copy(k, slot, send, *to):
        j = layer_of(*slot)
        return remote(ib_all.at[k, j], ib_all.at[k, j], send, ib_r.at[k, j], dev(z, *to))

    own, pair, by_y, by_x, diagonal = (y, c, x), (y, oc, x), (oy, c, x), (y, c, ox), (oy, c, ox)
    ib_copies = [
        ib_copy(k, own, ib_s.at[k, n], *to) for k in range(PARTS) for n, to in enumerate((by_x, by_y, pair))
    ]
    for copy in ib_copies:
        copy.start()

    def pt_recv(k):
        j = (me + k) % LAYER
        return remote(pt_all.at[j], pt_all.at[j], pt_s.at[j], pt_r.at[j], layer_dev(j))

    for k in range(1, LAYER):
        pt_recv(k).wait_recv()

    td_copies[1].wait_recv()
    td_send[2] = (td_acc[ahead] + td_recv[1].astype(F32)).astype(BF16)
    td_copies[2].start()

    share = pt_all.shape[2]
    turned_all = jnp.concatenate([pt_all[j].reshape(LINE * share, rows) for j in range(LAYER)], axis=1)

    def weight_copy(k, n):
        t = (z + n) % LINE
        return remote(wp_send.at[k, t], wp_recv.at[k, z], wp_s.at[k, t], wp_r.at[k, z], dev(t, y, c, x))

    for step in range(PARTS + 2):
        k = step
        if k < PARTS:
            for n, slot in enumerate((by_x, by_y)):
                ib_copy(k, slot, ib_f.at[k, n], *pair).wait_recv()
                if k % 2 == n:
                    on = ib_copy(k, slot, ib_d.at[k], *(by_y if n == 0 else by_x))
                    on.start()
                    ib_copies.append(on)
                on = ib_copy(k, slot, ib_f.at[k, n], *pair)
                on.start()
                ib_copies.append(on)
        k = step - 1
        if 0 <= k < PARTS:
            on = ib_copy(k, diagonal, ib_f.at[k, 2], *pair)
            on.wait_recv()
            on.start()
            ib_copies.append(on)
        k = step - 2
        if k < 0:
            continue
        for slot in ((y, oc, x), (oy, oc, x), (y, oc, ox), (oy, oc, ox)):
            ib_copy(k, slot, ib_f.at[k, 0], *pair).wait_recv()
        product = jnp.dot(turned_all, ib_all[k].reshape(LAYER * rows, part), preferred_element_type=F32)
        for t in range(LINE):
            weight_own[k, t] = product[t * share : (t + 1) * share]
            wp_send[k, t] = product[t * share : (t + 1) * share].astype(BF16)
        for n in range(1, LINE):
            weight_copy(k, n).start()

    td_copies[0].wait_recv()
    td_copies[2].wait_recv()
    total = td_acc[here] + td_recv[0].astype(F32) + td_recv[2].astype(F32)
    unit = text_unit[...]
    text_out[...] = (total - unit * jnp.sum(unit * total, axis=-1, keepdims=True)) * text_inv

    total = loss_part[odd, c]
    for k, peer in enumerate(peers):
        slot = loss_recv.at[peer]
        remote(slot, slot, ls_s.at[k], ls_r.at[peer], peer_dev(*peer)).wait_recv()
        total += loss_recv[peer]
    loss_out[...] = total / (LINE * QUAD * rows)

    for k in range(PARTS):
        total = weight_own[k, z]
        for n in range(1, LINE):
            t = (z + n) % LINE
            slot = wp_recv.at[k, t]
            remote(slot, slot, wp_s.at[k, t], wp_r.at[k, t], dev(t, y, c, x)).wait_recv()
            total += wp_recv[k, t].astype(F32)
        weight_out[:, k * part : (k + 1) * part] = total / 64.0

    text_whole(y).wait_send()
    for copy in far_texts + text_passes + pos_copies + image_copies + [image_pass]:
        copy.wait_send()
    for copy in id_copies + [far_copy] + td_copies + loss_copies:
        copy.wait_send()
    for copy in ib_copies:
        copy.wait_send()
    for k in range(1, LAYER):
        pt_copy(k).wait_send()
    for k in range(1, LINE):
        for part in range(PARTS):
            weight_copy(part, k).wait_send()


def fused(pooled, w_img, text_emb, pos_index, log_scale, bias):
    _, rows, width = pooled.shape
    emb = w_img.shape[1]
    share = width // (LINE * LAYER)
    vmem, dma = pltpu.VMEM, pltpu.SemaphoreType.DMA
    in_vmem = pl.BlockSpec(memory_space=pltpu.VMEM)
    in_hbm = pl.BlockSpec(memory_space=pltpu.HBM)
    in_smem = pl.BlockSpec(memory_space=pltpu.SMEM)
    block = (rows, emb)
    loss, weight, text = pl.pallas_call(
        fused_kernel,
        out_shape=(
            jax.ShapeDtypeStruct((1, rows), F32),
            jax.ShapeDtypeStruct((share, emb), F32),
            jax.ShapeDtypeStruct(block, F32),
        ),
        in_specs=[in_hbm, in_hbm, in_hbm, in_hbm, in_smem, in_smem],
        out_specs=(in_vmem, in_vmem, in_vmem),
        scratch_shapes=[
            vmem((rows, width), BF16),
            vmem((width, emb), BF16),
            vmem(block, BF16),
            vmem((1, rows), jnp.int32),
            vmem((2, 2) + block, BF16),
            vmem((2, 2) + block, BF16),
            vmem((2, 2, 1, rows), jnp.int32),
            vmem((LAYER, LINE, share, rows), BF16),
            vmem((LAYER, LINE, share, rows), BF16),
            vmem(block, F32),
            vmem(block, F32),
            vmem((2, 2) + block, F32),
            vmem((3,) + block, BF16),
            vmem((3,) + block, BF16),
            vmem((2, 2) + block, F32),
            vmem((2,) + block, BF16),
            vmem((2,) + block, BF16),
            vmem(block, BF16),
            vmem(block, BF16),
            vmem((2, 2, rows, rows), BF16),
            vmem((2, 2, 1, rows), F32),
            vmem((2, 2, 1, rows), F32),
            vmem((PARTS, LAYER, rows, emb // PARTS), BF16),
            vmem((PARTS, LINE, share, emb // PARTS), F32),
            vmem((PARTS, LINE, share, emb // PARTS), BF16),
            vmem((PARTS, LINE, share, emb // PARTS), BF16),
            dma((4,)),
            dma((PIECES,)), dma((PIECES,)), dma, dma((2, 2, PIECES)),
            dma((3,)), dma((2, 2)),
            dma((3,)), dma((2, 2)),
            dma((LAYER,)), dma((LAYER,)),
            dma((3,)), dma((3,)),
            dma((3,)), dma((3,)),
            dma((3,)), dma((2, 2)),
            dma((PARTS, 3)), dma((PARTS, 3)), dma((PARTS,)), dma((PARTS, LAYER)),
            dma((PARTS, LINE)), dma((PARTS, LINE)),
        ],
        compiler_params=pltpu.CompilerParams(
            collective_id=0, has_side_effects=True, vmem_limit_bytes=61 * 2**20
        ),
    )(pooled[0], w_img, text_emb[0], pos_index, log_scale, bias)
    return loss, weight, text[None]


def normalize(rows):
    squares = jnp.sum(rows * rows, axis=-1, keepdims=True)
    inverse = lax.rsqrt(squares + 1e-06)
    return (rows * inverse, inverse)


def pair_terms(left, right, left_pos, right_start, scale_value, shift):
    logits = scale_value * jnp.dot(left, right.T, preferred_element_type=jnp.float32) + shift
    columns = right_start + jnp.arange(right.shape[0], dtype=jnp.int32)
    sign = jnp.where(left_pos[:, None] == columns[None, :], 1.0, -1.0).astype(jnp.float32)
    losses = jax.nn.softplus(-sign * logits)
    coeffs = (-sign * jax.nn.sigmoid(-sign * logits) * scale_value).astype(jnp.bfloat16)
    return (jnp.sum(losses, axis=1), coeffs)


def transpose_dot(coeffs, rows):
    return lax.dot_general(
        coeffs, rows, (((0,), (0,)), ((), ())), preferred_element_type=jnp.float32
    )


def plain(pooled, w_img, text_emb, pos_index, log_scale, bias):
    scale_value = jnp.exp(log_scale[0])
    shift = bias[0]
    features = pooled[0]
    my_pos = pos_index[0]
    row_count = features.shape[0]
    group_size = row_count * lax.axis_size("blk")
    my_start = lax.axis_index("blk") * row_count
    projected = jnp.dot(features, w_img, preferred_element_type=jnp.float32)
    image_unit, image_inv = normalize(projected)
    image_low = image_unit.astype(jnp.bfloat16)
    text_unit, text_inv = normalize(text_emb[0].astype(jnp.float32))
    text_low = text_unit.astype(jnp.bfloat16)
    piece = lax.all_gather(text_low, "blk", axis=0, tiled=True)
    row_sums, coeffs = pair_terms(image_low, piece, my_pos, jnp.int32(0), scale_value, shift)
    loss_total = row_sums
    image_dir = jnp.dot(coeffs, piece, preferred_element_type=jnp.float32)
    pieces = (
        lax.all_gather(image_low, "blk", axis=0, tiled=True),
        lax.all_gather(my_pos, "blk", axis=0, tiled=True),
    )
    row_sums, coeffs = pair_terms(pieces[0], text_low, pieces[1], my_start, scale_value, shift)
    text_dir = transpose_dot(coeffs, pieces[0])
    image_back = (
        (image_dir - image_unit * jnp.sum(image_unit * image_dir, axis=-1, keepdims=True))
        * image_inv
    ).astype(jnp.bfloat16)
    text_back = (
        text_dir - text_unit * jnp.sum(text_unit * text_dir, axis=-1, keepdims=True)
    ) * text_inv
    weight_part = transpose_dot(features, image_back)
    weight_sum = lax.psum_scatter(weight_part, ("blk", "rep"), scatter_dimension=0, tiled=True)
    return ((loss_total / group_size)[None], weight_sum / 64.0, text_back[None])


def solution(mesh):
    def shards(pooled, w_img, text_emb, pos_index, log_scale, bias):
        _, rows, width = pooled.shape
        fits = mesh.shape["blk"] == LINE * QUAD and mesh.shape["rep"] * QUAD == LAYER
        fits = fits and rows % 128 == 0 and width % (LINE * LAYER * 16) == 0
        return (fused if fits else plain)(pooled, w_img, text_emb, pos_index, log_scale, bias)

    return jax.shard_map(
        shards,
        mesh=mesh,
        in_specs=(P("rep", "blk", None), P(), P("rep", "blk", None), P("rep", "blk"), P(), P()),
        out_specs=(P("rep", "blk"), P(("blk", "rep"), None), P("rep", "blk", None)),
        check_vma=False,
    )
```

```python
import jax
import jax.numpy as jnp
from jax import lax
from jax.experimental import pallas as pl
from jax.experimental.pallas import tpu as pltpu
from jax.sharding import PartitionSpec as P

F32 = jnp.float32
BF16 = jnp.bfloat16
LINE = 4
QUAD = 4
LAYER = 8
PIECES = 4
PARTS = 4


def fused_kernel(
    pooled_hbm, w_hbm, text_hbm, pos_hbm, log_scale, bias,
    loss_out, weight_out, text_out,
    pooled, w, text_in, pos_in, text_all, image_all, pos_all, pt_send, pt_all,
    text_unit, image_unit, td_acc, td_send, td_recv, id_acc, id_send, id_recv, id_far, id_far_recv,
    coeff_parts, loss_part, loss_recv, ib_all, weight_own, wp_send, wp_recv,
    in_sem, tg_s, tg_f, tg_y, tg_r, ig_s, ig_r, pg_s, pg_r, pt_s, pt_r, td_s, td_r,
    id_s, id_r, ls_s, ls_r, ib_s, ib_f, ib_d, ib_r, wp_s, wp_r,
):
    blk, x = lax.axis_index("blk"), lax.axis_index("rep")
    z, y, c = blk // 4, (blk // 2) % 2, blk % 2
    rows, emb = text_in.shape
    oy, oc, ox = 1 - y, 1 - c, 1 - x

    def dev(zz, yy, cc, xx):
        return {"blk": zz * 4 + yy * 2 + cc, "rep": xx}

    def layer_of(yy, cc, xx):
        return yy * 4 + cc * 2 + xx

    def layer_dev(j):
        return dev(z, j // 4, (j // 2) % 2, j % 2)

    def remote(src, dst, send, recv, device):
        return pltpu.make_async_remote_copy(
            src_ref=src, dst_ref=dst, send_sem=send, recv_sem=recv,
            device_id=device, device_id_type=pl.DeviceIdType.MESH,
        )

    half, odd = z // 2, z % 2
    other_half, other_odd = 1 - half, 1 - odd
    z_far, z_near = other_half * 2 + odd, half * 2 + other_odd
    me = layer_of(y, c, x)

    ins = [(text_hbm, text_in), (pos_hbm, pos_in), (pooled_hbm, pooled), (w_hbm, w)]
    ins = [pltpu.make_async_copy(src, dst, in_sem.at[k]) for k, (src, dst) in enumerate(ins)]
    for copy in ins:
        copy.start()
    barrier = pltpu.get_barrier_semaphore()
    for k in range(1, LAYER):
        pl.semaphore_signal(barrier, inc=1, device_id=layer_dev((me + k) % LAYER), device_id_type=pl.DeviceIdType.MESH)
    for k in range(1, LINE):
        pl.semaphore_signal(
            barrier, inc=1, device_id=dev((z + k) % LINE, y, c, x), device_id_type=pl.DeviceIdType.MESH
        )
    pl.semaphore_signal(barrier, inc=1, device_id=dev(z_near, y, oc, x), device_id_type=pl.DeviceIdType.MESH)

    ins[0].wait()
    raw = text_in[...].astype(F32)
    text_inv = lax.rsqrt(jnp.sum(raw * raw, axis=-1, keepdims=True) + 1e-06)
    unit = raw * text_inv
    text_unit[...] = unit
    text_all[half, y] = unit.astype(BF16)
    ins[1].wait()
    pos_all[odd, c] = pos_in[...]
    pl.semaphore_wait(barrier, LAYER - 1 + LINE)

    piece = rows // PIECES

    def text_piece(hh, yy, k, send, *to):
        slot = text_all.at[hh, yy, pl.ds(k * piece, piece)]
        return remote(slot, slot, send, tg_r.at[hh, yy, k], dev(*to))

    far_texts = [text_piece(half, y, k, tg_s.at[k], z_far, y, c, x) for k in range(PIECES)]
    for copy in far_texts:
        copy.start()

    def text_whole(yy):
        slot = text_all.at[half, yy]
        return remote(slot, slot, tg_y, tg_r.at[half, yy, 0], dev(z, oy, c, x))

    text_whole(y).start()

    peers = [(odd, oc), (other_odd, c), (other_odd, oc)]

    def peer_dev(oo, cc):
        return dev(half * 2 + oo, y, cc, x)

    pos_copies = [
        remote(pos_all.at[odd, c], pos_all.at[odd, c], pg_s.at[k], pg_r.at[odd, c], peer_dev(*peer))
        for k, peer in enumerate(peers)
    ]
    for copy in pos_copies:
        copy.start()

    ins[2].wait()
    ins[3].wait()
    projected = jnp.dot(pooled[...], w[...], preferred_element_type=F32)
    image_inv = lax.rsqrt(jnp.sum(projected * projected, axis=-1, keepdims=True) + 1e-06)
    unit = projected * image_inv
    image_unit[...] = unit
    image_all[odd, c] = unit.astype(BF16)

    def image_copy(k, oo, cc, to):
        slot = image_all.at[oo, cc]
        return remote(slot, slot, ig_s.at[k], ig_r.at[oo, cc], peer_dev(*to))

    image_copies = [image_copy(k, odd, c, to) for k, to in enumerate(peers[:2])]
    image_copies[1].start()
    image_copies[0].start()

    turned = pooled[...].T.reshape(LINE, LAYER, -1, rows)
    for j in range(LAYER):
        for t in range(LINE):
            pt_send[j, t] = turned[t, j]
    pt_all[me] = pt_send[me]

    def pt_copy(k):
        j = (me + k) % LAYER
        return remote(pt_send.at[j], pt_all.at[me], pt_s.at[j], pt_r.at[me], layer_dev(j))

    scale = jnp.exp(jnp.full((1, 2 * rows), log_scale[0], F32))
    shift = bias[0]

    def pairs(owners, oo):
        text = jnp.concatenate([text_all[hh, yy] for hh, yy in owners], axis=0)
        images = image_all[oo].reshape(2 * rows, emb)
        pos = jnp.concatenate([pos_all[oo, 0], pos_all[oo, 1]], axis=1)
        dots = lax.dot_general(text, images, (((1,), (1,)), ((), ())), preferred_element_type=F32)
        logits = scale * dots + shift
        index = lax.broadcasted_iota(jnp.int32, (rows, 2 * rows), 0)
        index = jnp.concatenate([((hh * 2 + odd) * 4 + yy * 2 + c) * rows + index for hh, yy in owners], axis=0)
        sign = jnp.where(index == pos, 1.0, -1.0).astype(F32)
        value = -sign * logits
        losses = jnp.sum(
            jnp.maximum(value, 0.0) + jnp.log1p(jnp.exp(-jnp.abs(value))), axis=0, keepdims=True
        )
        coeffs = (-sign * jax.nn.sigmoid(value) * scale).astype(BF16)
        return text, images, coeffs, losses

    def text_terms(coeffs, images):
        return jnp.dot(coeffs, images, preferred_element_type=F32)

    def image_terms(coeffs, text):
        return lax.dot_general(coeffs, text, (((0,), (0,)), ((), ())), preferred_element_type=F32)

    here, by_y, ahead, across = (half, y), (half, oy), (other_half, y), (other_half, oy)

    for k, peer in enumerate(peers):
        remote(pos_all.at[peer], pos_all.at[peer], pg_s.at[k], pg_r.at[peer], peer_dev(*peer)).wait_recv()
    text_whole(oy).wait_recv()
    image_copy(0, odd, oc, peers[0]).wait_recv()
    text, images, coeffs, loss_here = pairs([here, by_y], odd)
    terms = text_terms(coeffs, images)
    td_acc[here] = terms[:rows]
    td_acc[by_y] = terms[rows:]
    id_acc[odd] = image_terms(coeffs, text).reshape(2, rows, emb)

    text_passes = []
    for k in range(PIECES):
        copy = text_piece(*ahead, k, tg_f.at[k], z, oy, c, x)
        copy.wait_recv()
        copy.start()
        text_passes.append(copy)
    text, images, coeffs, losses = pairs([ahead], odd)
    loss_here += losses
    td_acc[ahead] = text_terms(coeffs, images)
    id_acc[odd] += image_terms(coeffs, text).reshape(2, rows, emb)

    image_pass = image_copy(2, other_odd, c, peers[0])
    image_pass.wait_recv()
    image_pass.start()
    for k in range(1, LAYER):
        pt_copy(k).start()
    image_copy(0, other_odd, oc, peers[0]).wait_recv()
    text, images, coeffs, loss_near = pairs([here, by_y, ahead], other_odd)
    terms = text_terms(coeffs, images)
    td_send[0] = (td_acc[by_y] + terms[rows : 2 * rows]).astype(BF16)

    def td_copy(k, *to):
        return remote(td_send.at[k], td_recv.at[k], td_s.at[k], td_r.at[k], dev(*to))

    td_copies = [td_copy(0, z, oy, c, x), td_copy(1, z, oy, c, x), td_copy(2, z_far, y, c, x)]
    td_acc[here] += terms[:rows]
    td_acc[ahead] += terms[2 * rows :]
    id_acc[other_odd] = image_terms(coeffs, text).reshape(2, rows, emb)

    for k in range(PIECES):
        text_piece(*across, k, tg_f.at[k], z, oy, c, x).wait_recv()

    def image_sum(oo, cc):
        return id_acc[oo, cc] + image_terms(coeff_parts[oo, cc], text)

    pair = dev(z, y, oc, x)
    id_copies = [remote(id_send.at[k], id_recv.at[k], id_s.at[k], id_r.at[k], pair) for k in range(2)]
    text, images, coeffs, losses = pairs([across], other_odd)
    loss_near += losses
    for k in range(2):
        coeff_parts[other_odd, k] = coeffs[:, k * rows : (k + 1) * rows]
    id_send[1] = image_sum(other_odd, oc).astype(BF16)
    id_copies[1].start()
    id_acc[other_odd, c] = image_sum(other_odd, c)
    near_images, near_coeffs = images, coeffs
    text, images, coeffs, losses = pairs([across], odd)
    loss_here += losses
    for k in range(2):
        coeff_parts[odd, k] = coeffs[:, k * rows : (k + 1) * rows]
    id_send[0] = image_sum(odd, oc).astype(BF16)
    id_copies[0].start()
    for k in range(2):
        loss_part[odd, k] = loss_here[:, k * rows : (k + 1) * rows]
        loss_part[other_odd, k] = loss_near[:, k * rows : (k + 1) * rows]
    id_copies[1].wait_recv()
    id_far[...] = (id_acc[other_odd, c] + id_recv[1].astype(F32)).astype(BF16)
    rows_half = rows // 2
    halves = [pl.ds(0, rows_half), pl.ds(rows_half, rows_half)]
    far_copies = [
        remote(id_far.at[h], id_far_recv.at[h], id_s.at[2 + n], id_r.at[2 + n], dev(z_near, y, c, x))
        for n, h in enumerate(halves)
    ]
    for copy in far_copies:
        copy.start()
    td_send[1] = (text_terms(coeffs, images) + text_terms(near_coeffs, near_images)).astype(BF16)
    td_copies[1].start()
    near = image_sum(odd, c)
    loss_copies = [
        remote(loss_part.at[peer], loss_recv.at[odd, c], ls_s.at[k], ls_r.at[odd, c], peer_dev(*peer))
        for k, peer in enumerate(peers)
    ]
    for copy in loss_copies:
        copy.start()
    id_copies[0].wait_recv()
    near += id_recv[0].astype(F32)

    part = emb // PARTS
    own, by_y, by_x, diagonal = (y, c, x), (oy, c, x), (y, c, ox), (oy, c, ox)
    cuts = [(pl.ds(0, PARTS // 2), 0), (pl.ds(PARTS // 2, PARTS // 2), 0)]
    cuts += [(pl.ds(k, 1), 1) for k in range(PARTS)]

    def ib_copy(m, slot, send, *to):
        columns, n = cuts[m]
        j = layer_of(*slot)
        ref = ib_all.at[columns, j, halves[n]]
        return remote(ref, ref, send, ib_r.at[m, j], dev(z, *to))

    ib_copies = []
    for n in range(2):
        far_copies[n].wait_recv()
        lines = slice(n * rows_half, (n + 1) * rows_half)
        image_dir = near[lines] + id_far_recv[halves[n]].astype(F32)
        unit = image_unit[halves[n]]
        image_back = (
            (image_dir - unit * jnp.sum(unit * image_dir, axis=-1, keepdims=True)) * image_inv[lines]
        ).astype(BF16)
        for k in range(PARTS):
            ib_all[k, me, halves[n]] = image_back[:, k * part : (k + 1) * part]
        for m, cut in enumerate(cuts):
            if cut[1] != n:
                continue
            for to_n, to in enumerate((by_x, by_y, (y, oc, x))):
                copy = ib_copy(m, own, ib_s.at[m, to_n], *to)
                copy.start()
                ib_copies.append(copy)

    def pt_recv(k):
        j = (me + k) % LAYER
        return remote(pt_all.at[j], pt_all.at[j], pt_s.at[j], pt_r.at[j], layer_dev(j))

    for k in range(1, LAYER):
        pt_recv(k).wait_recv()

    td_copies[1].wait_recv()
    td_send[2] = (td_acc[ahead] + td_recv[1].astype(F32)).astype(BF16)
    td_copies[2].start()

    share = pt_all.shape[2]
    turned_all = jnp.concatenate([pt_all[j].reshape(LINE * share, rows) for j in range(LAYER)], axis=1)

    def weight_copy(k, n):
        t = (z + n) % LINE
        return remote(wp_send.at[k, t], wp_recv.at[k, z], wp_s.at[k, t], wp_r.at[k, z], dev(t, y, c, x))

    pair = (y, oc, x)
    for step in range(len(cuts) + 2):
        m = step
        if m < len(cuts):
            for n, slot in enumerate((by_x, by_y)):
                ib_copy(m, slot, ib_f.at[m, n], *pair).wait_recv()
                if m % 2 == n:
                    on = ib_copy(m, slot, ib_d.at[m], *(by_y if n == 0 else by_x))
                    on.start()
                    ib_copies.append(on)
                on = ib_copy(m, slot, ib_f.at[m, n], *pair)
                on.start()
                ib_copies.append(on)
        if m == len(cuts) - 1:
            td_copies[0].start()
        m = step - 1
        if 0 <= m < len(cuts):
            on = ib_copy(m, diagonal, ib_f.at[m, 2], *pair)
            on.wait_recv()
            on.start()
            ib_copies.append(on)
        m = step - 2
        if m < 0:
            continue
        for slot in ((y, oc, x), (oy, oc, x), (y, oc, ox), (oy, oc, ox)):
            ib_copy(m, slot, ib_f.at[m, 0], *pair).wait_recv()
        k = m - 2
        if k < 0:
            continue
        product = jnp.dot(turned_all, ib_all[k].reshape(LAYER * rows, part), preferred_element_type=F32)
        for t in range(LINE):
            weight_own[k, t] = product[t * share : (t + 1) * share]
            wp_send[k, t] = product[t * share : (t + 1) * share].astype(BF16)
        for n in range(1, LINE):
            weight_copy(k, n).start()

    td_copies[0].wait_recv()
    td_copies[2].wait_recv()
    total = td_acc[here] + td_recv[0].astype(F32) + td_recv[2].astype(F32)
    unit = text_unit[...]
    text_out[...] = (total - unit * jnp.sum(unit * total, axis=-1, keepdims=True)) * text_inv

    total = loss_part[odd, c]
    for k, peer in enumerate(peers):
        slot = loss_recv.at[peer]
        remote(slot, slot, ls_s.at[k], ls_r.at[peer], peer_dev(*peer)).wait_recv()
        total += loss_recv[peer]
    loss_out[...] = total / (LINE * QUAD * rows)

    for k in range(PARTS):
        total = weight_own[k, z]
        for n in range(1, LINE):
            t = (z + n) % LINE
            slot = wp_recv.at[k, t]
            remote(slot, slot, wp_s.at[k, t], wp_r.at[k, t], dev(t, y, c, x)).wait_recv()
            total += wp_recv[k, t].astype(F32)
        weight_out[:, k * part : (k + 1) * part] = total / 64.0

    text_whole(y).wait_send()
    for copy in far_texts + text_passes + pos_copies + image_copies + [image_pass]:
        copy.wait_send()
    for copy in id_copies + far_copies + td_copies + loss_copies:
        copy.wait_send()
    for copy in ib_copies:
        copy.wait_send()
    for k in range(1, LAYER):
        pt_copy(k).wait_send()
    for k in range(1, LINE):
        for part in range(PARTS):
            weight_copy(part, k).wait_send()


def settle_kernel(loss_in, weight_in, text_in, loss_out, weight_out, text_out, sems):
    pairs = [(text_in, text_out), (weight_in, weight_out), (loss_in, loss_out)]
    copies = [pltpu.make_async_copy(src, dst, sems.at[k]) for k, (src, dst) in enumerate(pairs)]
    for copy in copies:
        copy.start()
    for copy in copies:
        copy.wait()


def settle(*results):
    anywhere = pl.BlockSpec(memory_space=pl.ANY)
    return pl.pallas_call(
        settle_kernel,
        out_shape=tuple(jax.ShapeDtypeStruct(r.shape, r.dtype) for r in results),
        in_specs=[anywhere] * len(results),
        out_specs=(anywhere,) * len(results),
        scratch_shapes=[pltpu.SemaphoreType.DMA((len(results),))],
        compiler_params=pltpu.CompilerParams(vmem_limit_bytes=61 * 2**20),
    )(*results)


def fused(pooled, w_img, text_emb, pos_index, log_scale, bias):
    _, rows, width = pooled.shape
    emb = w_img.shape[1]
    share = width // (LINE * LAYER)
    vmem, dma = pltpu.VMEM, pltpu.SemaphoreType.DMA
    in_vmem = pl.BlockSpec(memory_space=pltpu.VMEM)
    in_hbm = pl.BlockSpec(memory_space=pltpu.HBM)
    in_smem = pl.BlockSpec(memory_space=pltpu.SMEM)
    block = (rows, emb)
    loss, weight, text = pl.pallas_call(
        fused_kernel,
        out_shape=(
            jax.ShapeDtypeStruct((1, rows), F32),
            jax.ShapeDtypeStruct((share, emb), F32),
            jax.ShapeDtypeStruct(block, F32),
        ),
        in_specs=[in_hbm, in_hbm, in_hbm, in_hbm, in_smem, in_smem],
        out_specs=(in_vmem, in_vmem, in_vmem),
        scratch_shapes=[
            vmem((rows, width), BF16),
            vmem((width, emb), BF16),
            vmem(block, BF16),
            vmem((1, rows), jnp.int32),
            vmem((2, 2) + block, BF16),
            vmem((2, 2) + block, BF16),
            vmem((2, 2, 1, rows), jnp.int32),
            vmem((LAYER, LINE, share, rows), BF16),
            vmem((LAYER, LINE, share, rows), BF16),
            vmem(block, F32),
            vmem(block, F32),
            vmem((2, 2) + block, F32),
            vmem((3,) + block, BF16),
            vmem((3,) + block, BF16),
            vmem((2, 2) + block, F32),
            vmem((2,) + block, BF16),
            vmem((2,) + block, BF16),
            vmem(block, BF16),
            vmem(block, BF16),
            vmem((2, 2, rows, rows), BF16),
            vmem((2, 2, 1, rows), F32),
            vmem((2, 2, 1, rows), F32),
            vmem((PARTS, LAYER, rows, emb // PARTS), BF16),
            vmem((PARTS, LINE, share, emb // PARTS), F32),
            vmem((PARTS, LINE, share, emb // PARTS), BF16),
            vmem((PARTS, LINE, share, emb // PARTS), BF16),
            dma((4,)),
            dma((PIECES,)), dma((PIECES,)), dma, dma((2, 2, PIECES)),
            dma((3,)), dma((2, 2)),
            dma((3,)), dma((2, 2)),
            dma((LAYER,)), dma((LAYER,)),
            dma((3,)), dma((3,)),
            dma((4,)), dma((4,)),
            dma((3,)), dma((2, 2)),
            dma((PARTS + 2, 3)), dma((PARTS + 2, 3)), dma((PARTS + 2,)), dma((PARTS + 2, LAYER)),
            dma((PARTS, LINE)), dma((PARTS, LINE)),
        ],
        compiler_params=pltpu.CompilerParams(
            collective_id=0, has_side_effects=True, vmem_limit_bytes=61 * 2**20
        ),
    )(pooled[0], w_img, text_emb[0], pos_index, log_scale, bias)
    loss, weight, text = settle(loss, weight, text)
    return loss, weight, text[None]


def normalize(rows):
    squares = jnp.sum(rows * rows, axis=-1, keepdims=True)
    inverse = lax.rsqrt(squares + 1e-06)
    return (rows * inverse, inverse)


def pair_terms(left, right, left_pos, right_start, scale_value, shift):
    logits = scale_value * jnp.dot(left, right.T, preferred_element_type=jnp.float32) + shift
    columns = right_start + jnp.arange(right.shape[0], dtype=jnp.int32)
    sign = jnp.where(left_pos[:, None] == columns[None, :], 1.0, -1.0).astype(jnp.float32)
    losses = jax.nn.softplus(-sign * logits)
    coeffs = (-sign * jax.nn.sigmoid(-sign * logits) * scale_value).astype(jnp.bfloat16)
    return (jnp.sum(losses, axis=1), coeffs)


def transpose_dot(coeffs, rows):
    return lax.dot_general(
        coeffs, rows, (((0,), (0,)), ((), ())), preferred_element_type=jnp.float32
    )


def plain(pooled, w_img, text_emb, pos_index, log_scale, bias):
    scale_value = jnp.exp(log_scale[0])
    shift = bias[0]
    features = pooled[0]
    my_pos = pos_index[0]
    row_count = features.shape[0]
    group_size = row_count * lax.axis_size("blk")
    my_start = lax.axis_index("blk") * row_count
    projected = jnp.dot(features, w_img, preferred_element_type=jnp.float32)
    image_unit, image_inv = normalize(projected)
    image_low = image_unit.astype(jnp.bfloat16)
    text_unit, text_inv = normalize(text_emb[0].astype(jnp.float32))
    text_low = text_unit.astype(jnp.bfloat16)
    piece = lax.all_gather(text_low, "blk", axis=0, tiled=True)
    row_sums, coeffs = pair_terms(image_low, piece, my_pos, jnp.int32(0), scale_value, shift)
    loss_total = row_sums
    image_dir = jnp.dot(coeffs, piece, preferred_element_type=jnp.float32)
    pieces = (
        lax.all_gather(image_low, "blk", axis=0, tiled=True),
        lax.all_gather(my_pos, "blk", axis=0, tiled=True),
    )
    row_sums, coeffs = pair_terms(pieces[0], text_low, pieces[1], my_start, scale_value, shift)
    text_dir = transpose_dot(coeffs, pieces[0])
    image_back = (
        (image_dir - image_unit * jnp.sum(image_unit * image_dir, axis=-1, keepdims=True))
        * image_inv
    ).astype(jnp.bfloat16)
    text_back = (
        text_dir - text_unit * jnp.sum(text_unit * text_dir, axis=-1, keepdims=True)
    ) * text_inv
    weight_part = transpose_dot(features, image_back)
    weight_sum = lax.psum_scatter(weight_part, ("blk", "rep"), scatter_dimension=0, tiled=True)
    return ((loss_total / group_size)[None], weight_sum / 64.0, text_back[None])


def solution(mesh):
    def shards(pooled, w_img, text_emb, pos_index, log_scale, bias):
        _, rows, width = pooled.shape
        fits = mesh.shape["blk"] == LINE * QUAD and mesh.shape["rep"] * QUAD == LAYER
        fits = fits and rows % 128 == 0 and width % (LINE * LAYER * 16) == 0
        return (fused if fits else plain)(pooled, w_img, text_emb, pos_index, log_scale, bias)

    return jax.shard_map(
        shards,
        mesh=mesh,
        in_specs=(P("rep", "blk", None), P(), P("rep", "blk", None), P("rep", "blk"), P(), P()),
        out_specs=(P("rep", "blk"), P(("blk", "rep"), None), P("rep", "blk", None)),
        check_vma=False,
    )
```

```python
import jax
import jax.numpy as jnp
from jax import lax
from jax.experimental import pallas as pl
from jax.experimental.pallas import tpu as pltpu
from jax.sharding import PartitionSpec as P

F32 = jnp.float32
BF16 = jnp.bfloat16
LINE = 4
QUAD = 4
LAYER = 8
PARTS = 4


def fused_kernel(
    pooled_hbm, w_hbm, text_hbm, pos_hbm, log_scale, bias,
    loss_out, weight_out, text_out,
    pooled, w, text_in, pos_in, text_all, image_all, pos_all, pt_send, pt_all,
    text_unit, image_unit, td_own, td_acc, td_send, td_recv, id_acc, id_send, id_recv, id_far, id_far_recv,
    coeff_parts, loss_part, loss_recv, ib_all, weight_own, wp_send, wp_recv,
    in_sem, tg_s, tg_f, tg_r, ig_s, ig_r, pg_s, pg_r, pt_s, pt_r, td_s, td_r,
    id_s, id_r, ls_s, ls_r, ib_s, ib_f, ib_d, ib_r, wp_s, wp_r,
):
    blk, x = lax.axis_index("blk"), lax.axis_index("rep")
    z, y, c = blk // 4, (blk // 2) % 2, blk % 2
    rows, emb = text_in.shape
    oy, oc, ox = 1 - y, 1 - c, 1 - x

    def dev(zz, yy, cc, xx):
        return {"blk": zz * 4 + yy * 2 + cc, "rep": xx}

    def layer_of(yy, cc, xx):
        return yy * 4 + cc * 2 + xx

    def layer_dev(j):
        return dev(z, j // 4, (j // 2) % 2, j % 2)

    def remote(src, dst, send, recv, device):
        return pltpu.make_async_remote_copy(
            src_ref=src, dst_ref=dst, send_sem=send, recv_sem=recv,
            device_id=device, device_id_type=pl.DeviceIdType.MESH,
        )

    q, me = y * 2 + c, layer_of(y, c, x)
    far = z // 2
    mid = z * (1 - far) + (LINE - 1 - z) * far

    def flip(base):
        return base + far * (LINE - 1 - 2 * base)

    order = [flip(mid), flip(1 - mid), flip(2), flip(3)]

    ins = [(text_hbm, text_in), (pos_hbm, pos_in), (pooled_hbm, pooled), (w_hbm, w)]
    ins = [pltpu.make_async_copy(src, dst, in_sem.at[k]) for k, (src, dst) in enumerate(ins)]
    for copy in ins:
        copy.start()
    barrier = pltpu.get_barrier_semaphore()
    for k in range(1, LAYER):
        pl.semaphore_signal(barrier, inc=1, device_id=layer_dev((me + k) % LAYER), device_id_type=pl.DeviceIdType.MESH)
    for k in range(1, LINE):
        pl.semaphore_signal(
            barrier, inc=1, device_id=dev((z + k) % LINE, y, c, x), device_id_type=pl.DeviceIdType.MESH
        )

    ins[0].wait()
    raw = text_in[...].astype(F32)
    text_inv = lax.rsqrt(jnp.sum(raw * raw, axis=-1, keepdims=True) + 1e-06)
    unit = raw * text_inv
    text_unit[...] = unit
    text_all[z] = unit.astype(BF16)
    ins[1].wait()
    pos_all[q] = pos_in[...]
    pl.semaphore_wait(barrier, LAYER - 1 + LINE - 1)

    own_a = remote(text_all.at[z], text_all.at[z], tg_s.at[0], tg_r.at[z], dev(flip(1 + mid), y, c, x))
    own_b = remote(text_all.at[z], text_all.at[z], tg_s.at[1], tg_r.at[z], dev(flip(0), y, c, x))
    own_a.start()

    @pl.when(mid == 1)
    def _():
        own_b.start()

    peers = [(y, oc), (oy, c), (oy, oc)]
    pos_copies = [
        remote(pos_all.at[q], pos_all.at[q], pg_s.at[k], pg_r.at[q], dev(z, yy, cc, x))
        for k, (yy, cc) in enumerate(peers)
    ]
    for copy in pos_copies:
        copy.start()

    ins[2].wait()
    ins[3].wait()
    projected = jnp.dot(pooled[...], w[...], preferred_element_type=F32)
    image_inv = lax.rsqrt(jnp.sum(projected * projected, axis=-1, keepdims=True) + 1e-06)
    unit = projected * image_inv
    image_unit[...] = unit
    image_all[q] = unit.astype(BF16)
    image_copies = [
        remote(image_all.at[q], image_all.at[q], ig_s.at[k], ig_r.at[q], dev(z, yy, cc, x))
        for k, (yy, cc) in enumerate(peers[:2])
    ]
    image_copies[1].start()
    image_copies[0].start()

    turned = pooled[...].T.reshape(LINE, LAYER, -1, rows)
    for j in range(LAYER):
        for t in range(LINE):
            pt_send[j, t] = turned[t, j]
    pt_all[me] = pt_send[me]

    def pt_copy(k):
        j = (me + k) % LAYER
        return remote(pt_send.at[j], pt_all.at[me], pt_s.at[j], pt_r.at[me], layer_dev(j))

    def forward(i):
        s = order[i]
        slot = text_all.at[s]
        return remote(slot, slot, tg_f.at[i], tg_r.at[s], dev(flip(2 if i == 1 else 0), y, c, x))

    def arrive(i):
        copy = forward(i)
        copy.wait_recv()

        @pl.when(mid == 1)
        def _():
            copy.start()

    arrive(1)

    @pl.when(mid == 1)
    def _():
        copy = forward(2)
        copy.wait_recv()
        copy.start()

    for k, (yy, cc) in enumerate(peers):
        qq = yy * 2 + cc
        remote(pos_all.at[qq], pos_all.at[qq], pg_s.at[k], pg_r.at[qq], dev(z, yy, cc, x)).wait_recv()

    def image_slot(k, yy, cc):
        slot = image_all.at[yy * 2 + cc]
        return remote(slot, slot, ig_s.at[k], ig_r.at[yy * 2 + cc], dev(z, y, oc, x))

    image_pass = image_slot(2, oy, c)
    image_pass.wait_recv()
    image_pass.start()
    image_slot(0, y, oc).wait_recv()
    image_slot(0, oy, oc).wait_recv()

    for k in range(1, LAYER):
        pt_copy(k).start()

    images = image_all[...].reshape(QUAD * rows, emb)
    pos = jnp.concatenate([pos_all[k] for k in range(QUAD)], axis=1)
    scale = jnp.exp(jnp.full((1, QUAD * rows), log_scale[0], F32))
    shift = bias[0]
    losses = jnp.zeros((1, QUAD * rows), F32)

    def text_dir_copy(i):
        to = (1 - mid, 1 + mid, 1 + 2 * mid)[i - 1]
        slot = (0, 2 - mid, 3 - 2 * mid)[i - 1]
        return remote(td_send.at[i], td_recv.at[slot], td_s.at[i], td_r.at[slot], dev(flip(to), y, c, x))

    def text_dir_wait(slot):
        remote(td_recv.at[slot], td_recv.at[slot], td_s.at[0], td_r.at[slot], dev(z, y, oc, x)).wait_recv()

    def text_dir_merge(i):
        @pl.when(mid == 1)
        def _():
            text_dir_wait(i)
            td_send[i] = (td_acc[i - 2] + td_recv[i].astype(F32)).astype(BF16)
            text_dir_copy(i).start()

    def text_dir_from_end(i):
        @pl.when(mid == 0)
        def _():
            td_send[i] = td_acc[i - 2].astype(BF16)
            text_dir_copy(i).start()

    for i in range(LINE):
        if i == 2:

            @pl.when(mid == 0)
            def _():
                forward(2).wait_recv()

        if i == 3:
            arrive(3)
        s = order[i]
        text = text_all[s]
        dots = lax.dot_general(text, images, (((1,), (1,)), ((), ())), preferred_element_type=F32)
        logits = scale * dots + shift
        owner = (s * QUAD + q) * rows + lax.broadcasted_iota(jnp.int32, (rows, QUAD * rows), 0)
        sign = jnp.where(owner == pos, 1.0, -1.0).astype(F32)
        value = -sign * logits
        losses += jnp.sum(
            jnp.maximum(value, 0.0) + jnp.log1p(jnp.exp(-jnp.abs(value))), axis=0, keepdims=True
        )
        coeffs = (-sign * jax.nn.sigmoid(value) * scale).astype(BF16)
        if i == LINE - 1:
            break
        text_part = jnp.dot(coeffs, images, preferred_element_type=F32)
        if i == 0:
            td_own[...] = text_part
        elif i == 1:
            td_send[1] = text_part.astype(BF16)
        else:
            td_acc[0] = text_part
            text_dir_from_end(2)
        image_part = lax.dot_general(
            coeffs, text, (((0,), (0,)), ((), ())), preferred_element_type=F32
        ).reshape(QUAD, rows, emb)
        if i == 0:
            id_acc[...] = image_part
        else:
            id_acc[...] += image_part

    for k in range(QUAD):
        coeff_parts[k] = coeffs[:, k * rows : (k + 1) * rows]
        loss_part[k] = losses[:, k * rows : (k + 1) * rows]

    def image_sum(yy, cc):
        return id_acc[yy * 2 + cc] + lax.dot_general(
            coeff_parts[yy * 2 + cc], text, (((0,), (0,)), ((), ())), preferred_element_type=F32
        )

    pair = dev(z, y, oc, x)
    id_copies = [remote(id_send.at[k], id_recv.at[k], id_s.at[k], id_r.at[k], pair) for k in range(2)]
    id_send[1] = image_sum(oy, oc).astype(BF16)
    id_copies[1].start()
    id_send[0] = image_sum(y, oc).astype(BF16)
    id_copies[0].start()
    id_acc[oy * 2 + c] = image_sum(oy, c)
    id_copies[1].wait_recv()
    id_far[...] = (id_acc[oy * 2 + c] + id_recv[1].astype(F32)).astype(BF16)
    rows_half = rows // 2
    halves = [pl.ds(0, rows_half), pl.ds(rows_half, rows_half)]
    far_copies = [
        remote(id_far.at[h], id_far_recv.at[h], id_s.at[2 + n], id_r.at[2 + n], dev(z, oy, c, x))
        for n, h in enumerate(halves)
    ]
    for copy in far_copies:
        copy.start()
    near = image_sum(y, c)
    td_acc[1] = jnp.dot(coeffs, images, preferred_element_type=F32)
    text_dir_from_end(3)

    @pl.when(mid == 1)
    def _():
        text_dir_copy(1).start()

    loss_copies = [
        remote(loss_part.at[yy * 2 + cc], loss_recv.at[q], ls_s.at[k], ls_r.at[q], dev(z, yy, cc, x))
        for k, (yy, cc) in enumerate(peers)
    ]
    for copy in loss_copies:
        copy.start()
    id_copies[0].wait_recv()
    near += id_recv[0].astype(F32)

    part = emb // PARTS
    own, by_y, by_x, diagonal = (y, c, x), (oy, c, x), (y, c, ox), (oy, c, ox)
    cuts = [(pl.ds(0, PARTS // 2), 0), (pl.ds(PARTS // 2, PARTS // 2), 0)]
    cuts += [(pl.ds(k, 1), 1) for k in range(PARTS)]

    def ib_copy(m, slot, send, *to):
        columns, n = cuts[m]
        j = layer_of(*slot)
        ref = ib_all.at[columns, j, halves[n]]
        return remote(ref, ref, send, ib_r.at[m, j], dev(z, *to))

    text_dir_merge(2)
    ib_copies = []
    for n in range(2):
        far_copies[n].wait_recv()
        lines = slice(n * rows_half, (n + 1) * rows_half)
        image_dir = near[lines] + id_far_recv[halves[n]].astype(F32)
        unit = image_unit[halves[n]]
        image_back = (
            (image_dir - unit * jnp.sum(unit * image_dir, axis=-1, keepdims=True)) * image_inv[lines]
        ).astype(BF16)
        for k in range(PARTS):
            ib_all[k, me, halves[n]] = image_back[:, k * part : (k + 1) * part]
        for m, cut in enumerate(cuts):
            if cut[1] != n:
                continue
            for to_n, to in enumerate((by_x, by_y, (y, oc, x))):
                copy = ib_copy(m, own, ib_s.at[m, to_n], *to)
                copy.start()
                ib_copies.append(copy)

    def pt_recv(k):
        j = (me + k) % LAYER
        return remote(pt_all.at[j], pt_all.at[j], pt_s.at[j], pt_r.at[j], layer_dev(j))

    for k in range(1, LAYER):
        pt_recv(k).wait_recv()

    text_dir_merge(3)

    @pl.when(mid == 0)
    def _():
        text_dir_copy(1).start()

    share = pt_all.shape[2]
    turned_all = jnp.concatenate([pt_all[j].reshape(LINE * share, rows) for j in range(LAYER)], axis=1)

    def weight_copy(k, n):
        t = (z + n) % LINE
        return remote(wp_send.at[k, t], wp_recv.at[k, z], wp_s.at[k, t], wp_r.at[k, z], dev(t, y, c, x))

    pair = (y, oc, x)
    for step in range(len(cuts) + 2):
        m = step
        if m < len(cuts):
            for n, slot in enumerate((by_x, by_y)):
                ib_copy(m, slot, ib_f.at[m, n], *pair).wait_recv()
                if m % 2 == n:
                    on = ib_copy(m, slot, ib_d.at[m], *(by_y if n == 0 else by_x))
                    on.start()
                    ib_copies.append(on)
                on = ib_copy(m, slot, ib_f.at[m, n], *pair)
                on.start()
                ib_copies.append(on)
        m = step - 1
        if 0 <= m < len(cuts):
            on = ib_copy(m, diagonal, ib_f.at[m, 2], *pair)
            on.wait_recv()
            on.start()
            ib_copies.append(on)
        m = step - 2
        if m < 0:
            continue
        for slot in ((y, oc, x), (oy, oc, x), (y, oc, ox), (oy, oc, ox)):
            ib_copy(m, slot, ib_f.at[m, 0], *pair).wait_recv()
        k = m - 2
        if k < 0:
            continue
        product = jnp.dot(turned_all, ib_all[k].reshape(LAYER * rows, part), preferred_element_type=F32)
        for t in range(LINE):
            weight_own[k, t] = product[t * share : (t + 1) * share]
            wp_send[k, t] = product[t * share : (t + 1) * share].astype(BF16)
        for n in range(1, LINE):
            weight_copy(k, n).start()

    text_dir_wait(0)
    text_dir_wait(1)
    total = td_own[...] + td_recv[0].astype(F32) + td_recv[1].astype(F32)
    unit = text_unit[...]
    text_out[...] = (total - unit * jnp.sum(unit * total, axis=-1, keepdims=True)) * text_inv

    total = loss_part[q]
    for k, (yy, cc) in enumerate(peers):
        qq = yy * 2 + cc
        remote(loss_recv.at[qq], loss_recv.at[qq], ls_s.at[k], ls_r.at[qq], dev(z, yy, cc, x)).wait_recv()
        total += loss_recv[qq]
    loss_out[...] = total / (LINE * QUAD * rows)

    for k in range(PARTS):
        total = weight_own[k, z]
        for n in range(1, LINE):
            t = (z + n) % LINE
            slot = wp_recv.at[k, t]
            remote(slot, slot, wp_s.at[k, t], wp_r.at[k, t], dev(t, y, c, x)).wait_recv()
            total += wp_recv[k, t].astype(F32)
        weight_out[:, k * part : (k + 1) * part] = total / 64.0

    own_a.wait_send()

    @pl.when(mid == 1)
    def _():
        own_b.wait_send()
        for i in range(1, LINE):
            forward(i).wait_send()

    for copy in pos_copies + image_copies + [image_pass] + id_copies + far_copies + loss_copies:
        copy.wait_send()
    for copy in ib_copies:
        copy.wait_send()
    for k in range(1, LAYER):
        pt_copy(k).wait_send()
    for k in range(1, LINE):
        text_dir_copy(k).wait_send()
        for part in range(PARTS):
            weight_copy(part, k).wait_send()


def settle_kernel(loss_in, weight_in, text_in, loss_out, weight_out, text_out):
    loss_out[...] = loss_in[...]
    weight_out[...] = weight_in[...]
    text_out[...] = text_in[...]


def settle(*results):
    in_vmem = pl.BlockSpec(memory_space=pltpu.VMEM)
    return pl.pallas_call(
        settle_kernel,
        out_shape=tuple(jax.ShapeDtypeStruct(r.shape, r.dtype) for r in results),
        in_specs=[in_vmem] * len(results),
        out_specs=(in_vmem,) * len(results),
        compiler_params=pltpu.CompilerParams(vmem_limit_bytes=61 * 2**20),
    )(*results)


def fused(pooled, w_img, text_emb, pos_index, log_scale, bias):
    _, rows, width = pooled.shape
    emb = w_img.shape[1]
    share = width // (LINE * LAYER)
    vmem, dma = pltpu.VMEM, pltpu.SemaphoreType.DMA
    in_vmem = pl.BlockSpec(memory_space=pltpu.VMEM)
    in_hbm = pl.BlockSpec(memory_space=pltpu.HBM)
    in_smem = pl.BlockSpec(memory_space=pltpu.SMEM)
    block = (rows, emb)
    loss, weight, text = pl.pallas_call(
        fused_kernel,
        out_shape=(
            jax.ShapeDtypeStruct((1, rows), F32),
            jax.ShapeDtypeStruct((share, emb), F32),
            jax.ShapeDtypeStruct(block, F32),
        ),
        in_specs=[in_hbm, in_hbm, in_hbm, in_hbm, in_smem, in_smem],
        out_specs=(in_vmem, in_vmem, in_vmem),
        scratch_shapes=[
            vmem((rows, width), BF16),
            vmem((width, emb), BF16),
            vmem(block, BF16),
            vmem((1, rows), jnp.int32),
            vmem((LINE,) + block, BF16),
            vmem((QUAD,) + block, BF16),
            vmem((QUAD, 1, rows), jnp.int32),
            vmem((LAYER, LINE, share, rows), BF16),
            vmem((LAYER, LINE, share, rows), BF16),
            vmem(block, F32),
            vmem(block, F32),
            vmem(block, F32),
            vmem((2,) + block, F32),
            vmem((LINE,) + block, BF16),
            vmem((LINE,) + block, BF16),
            vmem((QUAD,) + block, F32),
            vmem((2,) + block, BF16),
            vmem((2,) + block, BF16),
            vmem(block, BF16),
            vmem(block, BF16),
            vmem((QUAD, rows, rows), BF16),
            vmem((QUAD, 1, rows), F32),
            vmem((QUAD, 1, rows), F32),
            vmem((PARTS, LAYER, rows, emb // PARTS), BF16),
            vmem((PARTS, LINE, share, emb // PARTS), F32),
            vmem((PARTS, LINE, share, emb // PARTS), BF16),
            vmem((PARTS, LINE, share, emb // PARTS), BF16),
            dma((4,)),
            dma((2,)), dma((LINE,)), dma((LINE,)),
            dma((3,)), dma((QUAD,)),
            dma((3,)), dma((QUAD,)),
            dma((LAYER,)), dma((LAYER,)),
            dma((LINE,)), dma((LINE,)),
            dma((4,)), dma((4,)),
            dma((3,)), dma((QUAD,)),
            dma((PARTS + 2, 3)), dma((PARTS + 2, 3)), dma((PARTS + 2,)), dma((PARTS + 2, LAYER)),
            dma((PARTS, LINE)), dma((PARTS, LINE)),
        ],
        compiler_params=pltpu.CompilerParams(
            collective_id=0, has_side_effects=True, vmem_limit_bytes=63 * 2**20
        ),
    )(pooled[0], w_img, text_emb[0], pos_index, log_scale, bias)
    loss, weight, text = settle(loss, weight, text)
    return loss, weight, text[None]


def normalize(rows):
    squares = jnp.sum(rows * rows, axis=-1, keepdims=True)
    inverse = lax.rsqrt(squares + 1e-06)
    return (rows * inverse, inverse)


def pair_terms(left, right, left_pos, right_start, scale_value, shift):
    logits = scale_value * jnp.dot(left, right.T, preferred_element_type=jnp.float32) + shift
    columns = right_start + jnp.arange(right.shape[0], dtype=jnp.int32)
    sign = jnp.where(left_pos[:, None] == columns[None, :], 1.0, -1.0).astype(jnp.float32)
    losses = jax.nn.softplus(-sign * logits)
    coeffs = (-sign * jax.nn.sigmoid(-sign * logits) * scale_value).astype(jnp.bfloat16)
    return (jnp.sum(losses, axis=1), coeffs)


def transpose_dot(coeffs, rows):
    return lax.dot_general(
        coeffs, rows, (((0,), (0,)), ((), ())), preferred_element_type=jnp.float32
    )


def plain(pooled, w_img, text_emb, pos_index, log_scale, bias):
    scale_value = jnp.exp(log_scale[0])
    shift = bias[0]
    features = pooled[0]
    my_pos = pos_index[0]
    row_count = features.shape[0]
    group_size = row_count * lax.axis_size("blk")
    my_start = lax.axis_index("blk") * row_count
    projected = jnp.dot(features, w_img, preferred_element_type=jnp.float32)
    image_unit, image_inv = normalize(projected)
    image_low = image_unit.astype(jnp.bfloat16)
    text_unit, text_inv = normalize(text_emb[0].astype(jnp.float32))
    text_low = text_unit.astype(jnp.bfloat16)
    piece = lax.all_gather(text_low, "blk", axis=0, tiled=True)
    row_sums, coeffs = pair_terms(image_low, piece, my_pos, jnp.int32(0), scale_value, shift)
    loss_total = row_sums
    image_dir = jnp.dot(coeffs, piece, preferred_element_type=jnp.float32)
    pieces = (
        lax.all_gather(image_low, "blk", axis=0, tiled=True),
        lax.all_gather(my_pos, "blk", axis=0, tiled=True),
    )
    row_sums, coeffs = pair_terms(pieces[0], text_low, pieces[1], my_start, scale_value, shift)
    text_dir = transpose_dot(coeffs, pieces[0])
    image_back = (
        (image_dir - image_unit * jnp.sum(image_unit * image_dir, axis=-1, keepdims=True))
        * image_inv
    ).astype(jnp.bfloat16)
    text_back = (
        text_dir - text_unit * jnp.sum(text_unit * text_dir, axis=-1, keepdims=True)
    ) * text_inv
    weight_part = transpose_dot(features, image_back)
    weight_sum = lax.psum_scatter(weight_part, ("blk", "rep"), scatter_dimension=0, tiled=True)
    return ((loss_total / group_size)[None], weight_sum / 64.0, text_back[None])


def solution(mesh):
    def shards(pooled, w_img, text_emb, pos_index, log_scale, bias):
        _, rows, width = pooled.shape
        fits = mesh.shape["blk"] == LINE * QUAD and mesh.shape["rep"] * QUAD == LAYER
        fits = fits and rows % 128 == 0 and width % (LINE * LAYER * 16) == 0
        return (fused if fits else plain)(pooled, w_img, text_emb, pos_index, log_scale, bias)

    return jax.shard_map(
        shards,
        mesh=mesh,
        in_specs=(P("rep", "blk", None), P(), P("rep", "blk", None), P("rep", "blk"), P(), P()),
        out_specs=(P("rep", "blk"), P(("blk", "rep"), None), P("rep", "blk", None)),
        check_vma=False,
    )
```

```python
import jax
import jax.numpy as jnp
from jax import lax
from jax.experimental import pallas as pl
from jax.experimental.pallas import tpu as pltpu
from jax.sharding import PartitionSpec as P

F32 = jnp.float32
BF16 = jnp.bfloat16
LINE = 4
QUAD = 4
LAYER = 8
PARTS = 4


def fused_kernel(
    pooled_hbm, w_hbm, text_hbm, pos_hbm, log_scale, bias,
    loss_out, weight_out, text_out,
    pooled, w, text_in, pos_in, text_all, image_all, pos_all, pt_send, pt_all,
    text_unit, image_unit, td_own, td_acc, td_send, td_recv, id_acc, id_send, id_recv, id_far, id_far_recv,
    coeff_parts, loss_part, loss_recv, ib_all, weight_own, wp_send, wp_recv,
    in_sem, tg_s, tg_f, tg_r, ig_s, ig_r, pg_s, pg_r, pt_s, pt_r, td_s, td_r,
    id_s, id_r, ls_s, ls_r, ib_s, ib_d, ib_r, wp_s, wp_r,
):
    blk, x = lax.axis_index("blk"), lax.axis_index("rep")
    z, y, c = blk // 4, (blk // 2) % 2, blk % 2
    rows, emb = text_in.shape
    oy, oc, ox = 1 - y, 1 - c, 1 - x

    def dev(zz, yy, cc, xx):
        return {"blk": zz * 4 + yy * 2 + cc, "rep": xx}

    def layer_of(yy, cc, xx):
        return yy * 4 + cc * 2 + xx

    def layer_dev(j):
        return dev(z, j // 4, (j // 2) % 2, j % 2)

    def remote(src, dst, send, recv, device):
        return pltpu.make_async_remote_copy(
            src_ref=src, dst_ref=dst, send_sem=send, recv_sem=recv,
            device_id=device, device_id_type=pl.DeviceIdType.MESH,
        )

    q, me = y * 2 + c, layer_of(y, c, x)
    far = z // 2
    mid = z * (1 - far) + (LINE - 1 - z) * far

    def flip(base):
        return base + far * (LINE - 1 - 2 * base)

    order = [flip(mid), flip(1 - mid), flip(2), flip(3)]

    ins = [(text_hbm, text_in), (pos_hbm, pos_in), (pooled_hbm, pooled), (w_hbm, w)]
    ins = [pltpu.make_async_copy(src, dst, in_sem.at[k]) for k, (src, dst) in enumerate(ins)]
    for copy in ins:
        copy.start()
    barrier = pltpu.get_barrier_semaphore()
    for k in range(1, LAYER):
        pl.semaphore_signal(barrier, inc=1, device_id=layer_dev((me + k) % LAYER), device_id_type=pl.DeviceIdType.MESH)
    for k in range(1, LINE):
        for cc in (c, oc):
            pl.semaphore_signal(
                barrier, inc=1, device_id=dev((z + k) % LINE, y, cc, x), device_id_type=pl.DeviceIdType.MESH
            )

    ins[0].wait()
    raw = text_in[...].astype(F32)
    text_inv = lax.rsqrt(jnp.sum(raw * raw, axis=-1, keepdims=True) + 1e-06)
    unit = raw * text_inv
    text_unit[...] = unit
    text_all[z] = unit.astype(BF16)
    ins[1].wait()
    pos_all[q] = pos_in[...]
    pl.semaphore_wait(barrier, LAYER - 1 + 2 * (LINE - 1))

    own_a = remote(text_all.at[z], text_all.at[z], tg_s.at[0], tg_r.at[z], dev(flip(1 + mid), y, c, x))
    own_b = remote(text_all.at[z], text_all.at[z], tg_s.at[1], tg_r.at[z], dev(flip(0), y, c, x))
    own_a.start()

    @pl.when(mid == 1)
    def _():
        own_b.start()

    peers = [(y, oc), (oy, c), (oy, oc)]
    pos_copies = [
        remote(pos_all.at[q], pos_all.at[q], pg_s.at[k], pg_r.at[q], dev(z, yy, cc, x))
        for k, (yy, cc) in enumerate(peers)
    ]
    for copy in pos_copies:
        copy.start()

    ins[2].wait()
    ins[3].wait()
    projected = jnp.dot(pooled[...], w[...], preferred_element_type=F32)
    image_inv = lax.rsqrt(jnp.sum(projected * projected, axis=-1, keepdims=True) + 1e-06)
    unit = projected * image_inv
    image_unit[...] = unit
    image_all[q] = unit.astype(BF16)
    image_copies = [
        remote(image_all.at[q], image_all.at[q], ig_s.at[k], ig_r.at[q], dev(z, yy, cc, x))
        for k, (yy, cc) in enumerate(peers[:2])
    ]
    image_copies[1].start()
    image_copies[0].start()

    turned = pooled[...].T.reshape(LINE, LAYER, -1, rows)
    for j in range(LAYER):
        for t in range(LINE):
            pt_send[j // 4, j % 2, (j // 2) % 2, t] = turned[t, j]
    pt_all[y, x] = pt_send[y, x]
    same_core = [(oy, x), (y, ox), (oy, ox)]

    def pt_copy(k):
        to = same_core[k]
        return remote(pt_send.at[to], pt_all.at[y, x], pt_s.at[k], pt_r.at[y, x], dev(z, to[0], c, to[1]))

    def forward(i):
        s = order[i]
        slot = text_all.at[s]
        return remote(slot, slot, tg_f.at[i], tg_r.at[s], dev(flip(2 if i == 1 else 0), y, c, x))

    def arrive(i):
        copy = forward(i)
        copy.wait_recv()

        @pl.when(mid == 1)
        def _():
            copy.start()

    arrive(1)

    @pl.when(mid == 1)
    def _():
        copy = forward(2)
        copy.wait_recv()
        copy.start()

    for k, (yy, cc) in enumerate(peers):
        qq = yy * 2 + cc
        remote(pos_all.at[qq], pos_all.at[qq], pg_s.at[k], pg_r.at[qq], dev(z, yy, cc, x)).wait_recv()

    def image_slot(k, yy, cc):
        slot = image_all.at[yy * 2 + cc]
        return remote(slot, slot, ig_s.at[k], ig_r.at[yy * 2 + cc], dev(z, y, oc, x))

    image_pass = image_slot(2, oy, c)
    image_pass.wait_recv()
    image_pass.start()
    image_slot(0, y, oc).wait_recv()
    image_slot(0, oy, oc).wait_recv()

    for k in range(3):
        pt_copy(k).start()

    images = image_all[...].reshape(QUAD * rows, emb)
    pos = jnp.concatenate([pos_all[k] for k in range(QUAD)], axis=1)
    scale = jnp.exp(jnp.full((1, QUAD * rows), log_scale[0], F32))
    shift = bias[0]
    losses = jnp.zeros((1, QUAD * rows), F32)

    def text_dir_copy(i):
        to = (1 - mid, 1 + mid, 1 + 2 * mid)[i - 1]
        slot = (0, 2 - mid, 3 - 2 * mid)[i - 1]
        return remote(td_send.at[i], td_recv.at[slot], td_s.at[i], td_r.at[slot], dev(flip(to), y, c, x))

    def text_dir_wait(slot):
        remote(td_recv.at[slot], td_recv.at[slot], td_s.at[0], td_r.at[slot], dev(z, y, oc, x)).wait_recv()

    def text_dir_merge(i):
        @pl.when(mid == 1)
        def _():
            text_dir_wait(i)
            td_send[i] = (td_acc[i - 2] + td_recv[i].astype(F32)).astype(BF16)
            text_dir_copy(i).start()

    def text_dir_from_end(i):
        @pl.when(mid == 0)
        def _():
            td_send[i] = td_acc[i - 2].astype(BF16)
            text_dir_copy(i).start()

    for i in range(LINE):
        if i == 2:

            @pl.when(mid == 0)
            def _():
                forward(2).wait_recv()

        if i == 3:
            arrive(3)
        s = order[i]
        text = text_all[s]
        dots = lax.dot_general(text, images, (((1,), (1,)), ((), ())), preferred_element_type=F32)
        logits = scale * dots + shift
        owner = (s * QUAD + q) * rows + lax.broadcasted_iota(jnp.int32, (rows, QUAD * rows), 0)
        sign = jnp.where(owner == pos, 1.0, -1.0).astype(F32)
        value = -sign * logits
        losses += jnp.sum(
            jnp.maximum(value, 0.0) + jnp.log1p(jnp.exp(-jnp.abs(value))), axis=0, keepdims=True
        )
        coeffs = (-sign * jax.nn.sigmoid(value) * scale).astype(BF16)
        if i == LINE - 1:
            break
        text_part = jnp.dot(coeffs, images, preferred_element_type=F32)
        if i == 0:
            td_own[...] = text_part
        elif i == 1:
            td_send[1] = text_part.astype(BF16)
        else:
            td_acc[0] = text_part
            text_dir_from_end(2)
        image_part = lax.dot_general(
            coeffs, text, (((0,), (0,)), ((), ())), preferred_element_type=F32
        ).reshape(QUAD, rows, emb)
        if i == 0:
            id_acc[...] = image_part
        else:
            id_acc[...] += image_part

    for k in range(QUAD):
        coeff_parts[k] = coeffs[:, k * rows : (k + 1) * rows]
        loss_part[k] = losses[:, k * rows : (k + 1) * rows]

    def image_sum(yy, cc):
        return id_acc[yy * 2 + cc] + lax.dot_general(
            coeff_parts[yy * 2 + cc], text, (((0,), (0,)), ((), ())), preferred_element_type=F32
        )

    pair = dev(z, y, oc, x)
    id_copies = [remote(id_send.at[k], id_recv.at[k], id_s.at[k], id_r.at[k], pair) for k in range(2)]
    id_send[1] = image_sum(oy, oc).astype(BF16)
    id_copies[1].start()
    id_send[0] = image_sum(y, oc).astype(BF16)
    id_copies[0].start()
    id_acc[oy * 2 + c] = image_sum(oy, c)
    id_copies[1].wait_recv()
    id_far[...] = (id_acc[oy * 2 + c] + id_recv[1].astype(F32)).astype(BF16)
    rows_half = rows // 2
    halves = [pl.ds(0, rows_half), pl.ds(rows_half, rows_half)]
    far_copies = [
        remote(id_far.at[h], id_far_recv.at[h], id_s.at[2 + n], id_r.at[2 + n], dev(z, oy, c, x))
        for n, h in enumerate(halves)
    ]
    for copy in far_copies:
        copy.start()
    near = image_sum(y, c)
    td_acc[1] = jnp.dot(coeffs, images, preferred_element_type=F32)
    text_dir_from_end(3)

    @pl.when(mid == 1)
    def _():
        text_dir_copy(1).start()

    loss_copies = [
        remote(loss_part.at[yy * 2 + cc], loss_recv.at[q], ls_s.at[k], ls_r.at[q], dev(z, yy, cc, x))
        for k, (yy, cc) in enumerate(peers)
    ]
    for copy in loss_copies:
        copy.start()
    id_copies[0].wait_recv()
    near += id_recv[0].astype(F32)

    part = emb // PARTS
    own, by_y, by_x, diagonal = (y, c, x), (oy, c, x), (y, c, ox), (oy, c, ox)
    cuts = [(pl.ds(0, PARTS // 2), 0), (pl.ds(PARTS // 2, PARTS // 2), 0)]
    cuts += [(pl.ds(k, 1), 1) for k in range(PARTS)]

    def ib_copy(m, slot, send, *to):
        columns, n = cuts[m]
        j = slot[0] * 2 + slot[2]
        ref = ib_all.at[columns, j, halves[n]]
        return remote(ref, ref, send, ib_r.at[m, j], dev(z, *to))

    text_dir_merge(2)
    ib_copies = []
    for n in range(2):
        far_copies[n].wait_recv()
        lines = slice(n * rows_half, (n + 1) * rows_half)
        image_dir = near[lines] + id_far_recv[halves[n]].astype(F32)
        unit = image_unit[halves[n]]
        image_back = (
            (image_dir - unit * jnp.sum(unit * image_dir, axis=-1, keepdims=True)) * image_inv[lines]
        ).astype(BF16)
        for k in range(PARTS):
            ib_all[k, y * 2 + x, halves[n]] = image_back[:, k * part : (k + 1) * part]
        for m, cut in enumerate(cuts):
            if cut[1] != n:
                continue
            for to_n, to in enumerate((by_x, by_y)):
                copy = ib_copy(m, own, ib_s.at[m, to_n], *to)
                copy.start()
                ib_copies.append(copy)

    for k, slot in enumerate(same_core):
        remote(pt_all.at[slot], pt_all.at[slot], pt_s.at[k], pt_r.at[slot], dev(z, slot[0], c, slot[1])).wait_recv()

    text_dir_merge(3)

    @pl.when(mid == 0)
    def _():
        text_dir_copy(1).start()

    share = pt_all.shape[4]
    turned_all = jnp.concatenate(
        [pt_all[j // 2, j % 2].reshape(LAYER * share, rows) for j in range(QUAD)], axis=1
    )
    line = [(cc, (z + n) % LINE) for n in range(LINE) for cc in (c, oc)][1:]

    def weight_copy(k, n):
        cc, t = line[n]
        return remote(wp_send.at[k, cc, t], wp_recv.at[k, c, z], wp_s.at[k, n], wp_r.at[k, c, z], dev(t, y, cc, x))

    for step in range(len(cuts) + 1):
        m = step
        if m < len(cuts):
            for n, slot in enumerate((by_x, by_y)):
                to = by_y if n == 0 else by_x
                on = ib_copy(m, slot, ib_d.at[m], *to)
                on.wait_recv()
                if m % 2 == n:
                    on.start()
                    ib_copies.append(on)
        m = step - 1
        if m < 0:
            continue
        ib_copy(m, diagonal, ib_d.at[m], *by_y).wait_recv()
        k = m - 2
        if k < 0:
            continue
        product = jnp.dot(turned_all, ib_all[k].reshape(QUAD * rows, part), preferred_element_type=F32)
        product = product.reshape(2, LINE, share, part)
        weight_own[k] = product
        wp_send[k] = product.astype(BF16)
        for n in range(len(line)):
            weight_copy(k, n).start()

    text_dir_wait(0)
    text_dir_wait(1)
    total = td_own[...] + td_recv[0].astype(F32) + td_recv[1].astype(F32)
    unit = text_unit[...]
    text_out[...] = (total - unit * jnp.sum(unit * total, axis=-1, keepdims=True)) * text_inv

    total = loss_part[q]
    for k, (yy, cc) in enumerate(peers):
        qq = yy * 2 + cc
        remote(loss_recv.at[qq], loss_recv.at[qq], ls_s.at[k], ls_r.at[qq], dev(z, yy, cc, x)).wait_recv()
        total += loss_recv[qq]
    loss_out[...] = total / (LINE * QUAD * rows)

    for k in range(PARTS):
        total = weight_own[k, c, z]
        for n, (cc, t) in enumerate(line):
            slot = wp_recv.at[k, cc, t]
            remote(slot, slot, wp_s.at[k, n], wp_r.at[k, cc, t], dev(t, y, cc, x)).wait_recv()
            total += wp_recv[k, cc, t].astype(F32)
        weight_out[:, k * part : (k + 1) * part] = total / 64.0

    own_a.wait_send()

    @pl.when(mid == 1)
    def _():
        own_b.wait_send()
        for i in range(1, LINE):
            forward(i).wait_send()

    for copy in pos_copies + image_copies + [image_pass] + id_copies + far_copies + loss_copies:
        copy.wait_send()
    for copy in ib_copies:
        copy.wait_send()
    for k in range(3):
        pt_copy(k).wait_send()
        text_dir_copy(k + 1).wait_send()
    for part in range(PARTS):
        for n in range(len(line)):
            weight_copy(part, n).wait_send()


def settle_kernel(loss_in, weight_in, text_in, loss_out, weight_out, text_out):
    loss_out[...] = loss_in[...]
    weight_out[...] = weight_in[...]
    text_out[...] = text_in[...]


def settle(*results):
    in_vmem = pl.BlockSpec(memory_space=pltpu.VMEM)
    return pl.pallas_call(
        settle_kernel,
        out_shape=tuple(jax.ShapeDtypeStruct(r.shape, r.dtype) for r in results),
        in_specs=[in_vmem] * len(results),
        out_specs=(in_vmem,) * len(results),
        compiler_params=pltpu.CompilerParams(vmem_limit_bytes=61 * 2**20),
    )(*results)


def fused(pooled, w_img, text_emb, pos_index, log_scale, bias):
    _, rows, width = pooled.shape
    emb = w_img.shape[1]
    share = width // (LINE * LAYER)
    vmem, dma = pltpu.VMEM, pltpu.SemaphoreType.DMA
    in_vmem = pl.BlockSpec(memory_space=pltpu.VMEM)
    in_hbm = pl.BlockSpec(memory_space=pltpu.HBM)
    in_smem = pl.BlockSpec(memory_space=pltpu.SMEM)
    block = (rows, emb)
    loss, weight, text = pl.pallas_call(
        fused_kernel,
        out_shape=(
            jax.ShapeDtypeStruct((1, rows), F32),
            jax.ShapeDtypeStruct((share, emb), F32),
            jax.ShapeDtypeStruct(block, F32),
        ),
        in_specs=[in_hbm, in_hbm, in_hbm, in_hbm, in_smem, in_smem],
        out_specs=(in_vmem, in_vmem, in_vmem),
        scratch_shapes=[
            vmem((rows, width), BF16),
            vmem((width, emb), BF16),
            vmem(block, BF16),
            vmem((1, rows), jnp.int32),
            vmem((LINE,) + block, BF16),
            vmem((QUAD,) + block, BF16),
            vmem((QUAD, 1, rows), jnp.int32),
            vmem((2, 2, 2, LINE, share, rows), BF16),
            vmem((2, 2, 2, LINE, share, rows), BF16),
            vmem(block, F32),
            vmem(block, F32),
            vmem(block, F32),
            vmem((2,) + block, F32),
            vmem((LINE,) + block, BF16),
            vmem((LINE,) + block, BF16),
            vmem((QUAD,) + block, F32),
            vmem((2,) + block, BF16),
            vmem((2,) + block, BF16),
            vmem(block, BF16),
            vmem(block, BF16),
            vmem((QUAD, rows, rows), BF16),
            vmem((QUAD, 1, rows), F32),
            vmem((QUAD, 1, rows), F32),
            vmem((PARTS, QUAD, rows, emb // PARTS), BF16),
            vmem((PARTS, 2, LINE, share, emb // PARTS), F32),
            vmem((PARTS, 2, LINE, share, emb // PARTS), BF16),
            vmem((PARTS, 2, LINE, share, emb // PARTS), BF16),
            dma((4,)),
            dma((2,)), dma((LINE,)), dma((LINE,)),
            dma((3,)), dma((QUAD,)),
            dma((3,)), dma((QUAD,)),
            dma((3,)), dma((2, 2)),
            dma((LINE,)), dma((LINE,)),
            dma((4,)), dma((4,)),
            dma((3,)), dma((QUAD,)),
            dma((PARTS + 2, 2)), dma((PARTS + 2,)), dma((PARTS + 2, QUAD)),
            dma((PARTS, LAYER)), dma((PARTS, 2, LINE)),
        ],
        compiler_params=pltpu.CompilerParams(
            collective_id=0, has_side_effects=True, vmem_limit_bytes=63 * 2**20
        ),
    )(pooled[0], w_img, text_emb[0], pos_index, log_scale, bias)
    loss, weight, text = settle(loss, weight, text)
    return loss, weight, text[None]


def normalize(rows):
    squares = jnp.sum(rows * rows, axis=-1, keepdims=True)
    inverse = lax.rsqrt(squares + 1e-06)
    return (rows * inverse, inverse)


def pair_terms(left, right, left_pos, right_start, scale_value, shift):
    logits = scale_value * jnp.dot(left, right.T, preferred_element_type=jnp.float32) + shift
    columns = right_start + jnp.arange(right.shape[0], dtype=jnp.int32)
    sign = jnp.where(left_pos[:, None] == columns[None, :], 1.0, -1.0).astype(jnp.float32)
    losses = jax.nn.softplus(-sign * logits)
    coeffs = (-sign * jax.nn.sigmoid(-sign * logits) * scale_value).astype(jnp.bfloat16)
    return (jnp.sum(losses, axis=1), coeffs)


def transpose_dot(coeffs, rows):
    return lax.dot_general(
        coeffs, rows, (((0,), (0,)), ((), ())), preferred_element_type=jnp.float32
    )


def plain(pooled, w_img, text_emb, pos_index, log_scale, bias):
    scale_value = jnp.exp(log_scale[0])
    shift = bias[0]
    features = pooled[0]
    my_pos = pos_index[0]
    row_count = features.shape[0]
    group_size = row_count * lax.axis_size("blk")
    my_start = lax.axis_index("blk") * row_count
    projected = jnp.dot(features, w_img, preferred_element_type=jnp.float32)
    image_unit, image_inv = normalize(projected)
    image_low = image_unit.astype(jnp.bfloat16)
    text_unit, text_inv = normalize(text_emb[0].astype(jnp.float32))
    text_low = text_unit.astype(jnp.bfloat16)
    piece = lax.all_gather(text_low, "blk", axis=0, tiled=True)
    row_sums, coeffs = pair_terms(image_low, piece, my_pos, jnp.int32(0), scale_value, shift)
    loss_total = row_sums
    image_dir = jnp.dot(coeffs, piece, preferred_element_type=jnp.float32)
    pieces = (
        lax.all_gather(image_low, "blk", axis=0, tiled=True),
        lax.all_gather(my_pos, "blk", axis=0, tiled=True),
    )
    row_sums, coeffs = pair_terms(pieces[0], text_low, pieces[1], my_start, scale_value, shift)
    text_dir = transpose_dot(coeffs, pieces[0])
    image_back = (
        (image_dir - image_unit * jnp.sum(image_unit * image_dir, axis=-1, keepdims=True))
        * image_inv
    ).astype(jnp.bfloat16)
    text_back = (
        text_dir - text_unit * jnp.sum(text_unit * text_dir, axis=-1, keepdims=True)
    ) * text_inv
    weight_part = transpose_dot(features, image_back)
    weight_sum = lax.psum_scatter(weight_part, ("blk", "rep"), scatter_dimension=0, tiled=True)
    return ((loss_total / group_size)[None], weight_sum / 64.0, text_back[None])


def solution(mesh):
    def shards(pooled, w_img, text_emb, pos_index, log_scale, bias):
        _, rows, width = pooled.shape
        fits = mesh.shape["blk"] == LINE * QUAD and mesh.shape["rep"] * QUAD == LAYER
        fits = fits and rows % 128 == 0 and width % (LINE * LAYER * 16) == 0
        return (fused if fits else plain)(pooled, w_img, text_emb, pos_index, log_scale, bias)

    return jax.shard_map(
        shards,
        mesh=mesh,
        in_specs=(P("rep", "blk", None), P(), P("rep", "blk", None), P("rep", "blk"), P(), P()),
        out_specs=(P("rep", "blk"), P(("blk", "rep"), None), P("rep", "blk", None)),
        check_vma=False,
    )
```

```python
import jax
import jax.numpy as jnp
from jax import lax
from jax.experimental import pallas as pl
from jax.experimental.pallas import tpu as pltpu
from jax.sharding import PartitionSpec as P

F32 = jnp.float32
BF16 = jnp.bfloat16
LINE = 4
QUAD = 4
LAYER = 8
PARTS = 4


def fused_kernel(
    pooled_hbm, w_hbm, text_hbm, pos_hbm, log_scale, bias,
    loss_out, weight_out, text_out,
    pooled, w, text_in, pos_in, text_all, image_all, pos_all, pt_send, pt_all,
    text_unit, image_unit, td_own, td_acc, td_send, td_recv, id_acc, id_send, id_recv, id_far, id_far_recv,
    coeff_parts, loss_part, loss_recv, ib_all, weight_own, wp_send, wp_recv,
    in_sem, tg_s, tg_f, tg_r, ig_s, ig_r, pg_s, pg_r, pt_s, pt_r, td_s, td_r,
    id_s, id_r, ls_s, ls_r, ib_s, ib_f, ib_d, ib_r, wp_s, wp_r,
):
    blk, x = lax.axis_index("blk"), lax.axis_index("rep")
    z, y, c = blk // 4, (blk // 2) % 2, blk % 2
    rows, emb = text_in.shape
    oy, oc, ox = 1 - y, 1 - c, 1 - x

    def dev(zz, yy, cc, xx):
        return {"blk": zz * 4 + yy * 2 + cc, "rep": xx}

    def layer_of(yy, cc, xx):
        return yy * 4 + cc * 2 + xx

    def layer_dev(j):
        return dev(z, j // 4, (j // 2) % 2, j % 2)

    def remote(src, dst, send, recv, device):
        return pltpu.make_async_remote_copy(
            src_ref=src, dst_ref=dst, send_sem=send, recv_sem=recv,
            device_id=device, device_id_type=pl.DeviceIdType.MESH,
        )

    q, me = y * 2 + c, layer_of(y, c, x)
    far = z // 2
    mid = z * (1 - far) + (LINE - 1 - z) * far

    def flip(base):
        return base + far * (LINE - 1 - 2 * base)

    order = [flip(mid), flip(1 - mid), flip(2), flip(3)]

    ins = [(text_hbm, text_in), (pos_hbm, pos_in), (pooled_hbm, pooled), (w_hbm, w)]
    ins = [pltpu.make_async_copy(src, dst, in_sem.at[k]) for k, (src, dst) in enumerate(ins)]
    for copy in ins:
        copy.start()
    barrier = pltpu.get_barrier_semaphore()
    for k in range(1, LAYER):
        pl.semaphore_signal(barrier, inc=1, device_id=layer_dev((me + k) % LAYER), device_id_type=pl.DeviceIdType.MESH)
    for k in range(1, LINE):
        pl.semaphore_signal(
            barrier, inc=1, device_id=dev((z + k) % LINE, y, c, x), device_id_type=pl.DeviceIdType.MESH
        )

    ins[0].wait()
    raw = text_in[...].astype(F32)
    text_inv = lax.rsqrt(jnp.sum(raw * raw, axis=-1, keepdims=True) + 1e-06)
    unit = raw * text_inv
    text_unit[...] = unit
    text_all[z] = unit.astype(BF16)
    ins[1].wait()
    pos_all[q] = pos_in[...]
    pl.semaphore_wait(barrier, LAYER - 1 + LINE - 1)

    own_a = remote(text_all.at[z], text_all.at[z], tg_s.at[0], tg_r.at[z], dev(flip(1 + mid), y, c, x))
    own_b = remote(text_all.at[z], text_all.at[z], tg_s.at[1], tg_r.at[z], dev(flip(0), y, c, x))
    own_a.start()

    @pl.when(mid == 1)
    def _():
        own_b.start()

    peers = [(y, oc), (oy, c), (oy, oc)]
    pos_copies = [
        remote(pos_all.at[q], pos_all.at[q], pg_s.at[k], pg_r.at[q], dev(z, yy, cc, x))
        for k, (yy, cc) in enumerate(peers)
    ]
    for copy in pos_copies:
        copy.start()

    ins[2].wait()
    ins[3].wait()
    projected = jnp.dot(pooled[...], w[...], preferred_element_type=F32)
    image_inv = lax.rsqrt(jnp.sum(projected * projected, axis=-1, keepdims=True) + 1e-06)
    unit = projected * image_inv
    image_unit[...] = unit
    image_all[q] = unit.astype(BF16)
    image_copies = [
        remote(image_all.at[q], image_all.at[q], ig_s.at[k], ig_r.at[q], dev(z, yy, cc, x))
        for k, (yy, cc) in enumerate(peers[:2])
    ]
    image_copies[1].start()
    image_copies[0].start()

    turned = pooled[...].T.reshape(LINE, LAYER, -1, rows)
    for j in range(LAYER):
        for t in range(LINE):
            pt_send[j, t] = turned[t, j]
    pt_all[me] = pt_send[me]

    def pt_copy(k):
        j = (me + k) % LAYER
        return remote(pt_send.at[j], pt_all.at[me], pt_s.at[j], pt_r.at[me], layer_dev(j))

    def forward(i):
        s = order[i]
        slot = text_all.at[s]
        return remote(slot, slot, tg_f.at[i], tg_r.at[s], dev(flip(2 if i == 1 else 0), y, c, x))

    def arrive(i):
        copy = forward(i)
        copy.wait_recv()

        @pl.when(mid == 1)
        def _():
            copy.start()

    arrive(1)

    @pl.when(mid == 1)
    def _():
        copy = forward(2)
        copy.wait_recv()
        copy.start()

    for k, (yy, cc) in enumerate(peers):
        qq = yy * 2 + cc
        remote(pos_all.at[qq], pos_all.at[qq], pg_s.at[k], pg_r.at[qq], dev(z, yy, cc, x)).wait_recv()

    def image_slot(k, yy, cc):
        slot = image_all.at[yy * 2 + cc]
        return remote(slot, slot, ig_s.at[k], ig_r.at[yy * 2 + cc], dev(z, y, oc, x))

    image_pass = image_slot(2, oy, c)
    image_pass.wait_recv()
    image_pass.start()
    image_slot(0, y, oc).wait_recv()
    image_slot(0, oy, oc).wait_recv()

    for k in range(1, LAYER):
        pt_copy(k).start()

    images = image_all[...].reshape(QUAD * rows, emb)
    pos = jnp.concatenate([pos_all[k] for k in range(QUAD)], axis=1)
    scale = jnp.exp(jnp.full((1, QUAD * rows), log_scale[0], F32))
    shift = bias[0]
    losses = jnp.zeros((1, QUAD * rows), F32)

    def text_dir_copy(i):
        to = (1 - mid, 1 + mid, 1 + 2 * mid)[i - 1]
        slot = (0, 2 - mid, 3 - 2 * mid)[i - 1]
        return remote(td_send.at[i], td_recv.at[slot], td_s.at[i], td_r.at[slot], dev(flip(to), y, c, x))

    def text_dir_wait(slot):
        remote(td_recv.at[slot], td_recv.at[slot], td_s.at[0], td_r.at[slot], dev(z, y, oc, x)).wait_recv()

    def text_dir_merge(i):
        @pl.when(mid == 1)
        def _():
            text_dir_wait(i)
            td_send[i] = (td_acc[i - 2] + td_recv[i].astype(F32)).astype(BF16)
            text_dir_copy(i).start()

    def text_dir_from_end(i):
        @pl.when(mid == 0)
        def _():
            td_send[i] = td_acc[i - 2].astype(BF16)
            text_dir_copy(i).start()

    for i in range(LINE):
        if i == 2:

            @pl.when(mid == 0)
            def _():
                forward(2).wait_recv()

        if i == 3:
            arrive(3)
        s = order[i]
        text = text_all[s]
        dots = lax.dot_general(text, images, (((1,), (1,)), ((), ())), preferred_element_type=F32)
        logits = scale * dots + shift
        owner = (s * QUAD + q) * rows + lax.broadcasted_iota(jnp.int32, (rows, QUAD * rows), 0)
        sign = jnp.where(owner == pos, 1.0, -1.0).astype(F32)
        value = -sign * logits
        losses += jnp.sum(
            jnp.maximum(value, 0.0) + jnp.log1p(jnp.exp(-jnp.abs(value))), axis=0, keepdims=True
        )
        coeffs = (-sign * jax.nn.sigmoid(value) * scale).astype(BF16)
        if i == LINE - 1:
            break
        text_part = jnp.dot(coeffs, images, preferred_element_type=F32)
        if i == 0:
            td_own[...] = text_part
        elif i == 1:
            td_send[1] = text_part.astype(BF16)
        else:
            td_acc[0] = text_part
            text_dir_from_end(2)
        image_part = lax.dot_general(
            coeffs, text, (((0,), (0,)), ((), ())), preferred_element_type=F32
        ).reshape(QUAD, rows, emb)
        if i == 0:
            id_acc[...] = image_part
        else:
            id_acc[...] += image_part

    for k in range(QUAD):
        coeff_parts[k] = coeffs[:, k * rows : (k + 1) * rows]
        loss_part[k] = losses[:, k * rows : (k + 1) * rows]

    def image_sum(yy, cc):
        return id_acc[yy * 2 + cc] + lax.dot_general(
            coeff_parts[yy * 2 + cc], text, (((0,), (0,)), ((), ())), preferred_element_type=F32
        )

    pair = dev(z, y, oc, x)
    id_copies = [remote(id_send.at[k], id_recv.at[k], id_s.at[k], id_r.at[k], pair) for k in range(2)]
    id_send[1] = image_sum(oy, oc).astype(BF16)
    id_copies[1].start()
    id_send[0] = image_sum(y, oc).astype(BF16)
    id_copies[0].start()
    id_acc[oy * 2 + c] = image_sum(oy, c)
    id_copies[1].wait_recv()
    id_far[...] = (id_acc[oy * 2 + c] + id_recv[1].astype(F32)).astype(BF16)
    rows_half = rows // 2
    halves = [pl.ds(0, rows_half), pl.ds(rows_half, rows_half)]
    far_copies = [
        remote(id_far.at[h], id_far_recv.at[h], id_s.at[2 + n], id_r.at[2 + n], dev(z, oy, c, x))
        for n, h in enumerate(halves)
    ]
    for copy in far_copies:
        copy.start()
    near = image_sum(y, c)
    td_acc[1] = jnp.dot(coeffs, images, preferred_element_type=F32)
    text_dir_from_end(3)

    @pl.when(mid == 1)
    def _():
        text_dir_copy(1).start()

    loss_copies = [
        remote(loss_part.at[yy * 2 + cc], loss_recv.at[q], ls_s.at[k], ls_r.at[q], dev(z, yy, cc, x))
        for k, (yy, cc) in enumerate(peers)
    ]
    for copy in loss_copies:
        copy.start()
    id_copies[0].wait_recv()
    near += id_recv[0].astype(F32)

    part = emb // PARTS
    own, by_y, by_x, diagonal = (y, c, x), (oy, c, x), (y, c, ox), (oy, c, ox)
    cuts = [(pl.ds(0, PARTS // 2), 0), (pl.ds(PARTS // 2, PARTS // 2), 0)]
    cuts += [(pl.ds(k, 1), 1) for k in range(PARTS)]

    def ib_copy(m, slot, send, *to):
        columns, n = cuts[m]
        j = layer_of(*slot)
        ref = ib_all.at[columns, j, halves[n]]
        return remote(ref, ref, send, ib_r.at[m, j], dev(z, *to))

    text_dir_merge(2)
    ib_copies = []
    for n in range(2):
        far_copies[n].wait_recv()
        lines = slice(n * rows_half, (n + 1) * rows_half)
        image_dir = near[lines] + id_far_recv[halves[n]].astype(F32)
        unit = image_unit[halves[n]]
        image_back = (
            (image_dir - unit * jnp.sum(unit * image_dir, axis=-1, keepdims=True)) * image_inv[lines]
        ).astype(BF16)
        for k in range(PARTS):
            ib_all[k, me, halves[n]] = image_back[:, k * part : (k + 1) * part]
        for m, cut in enumerate(cuts):
            if cut[1] != n:
                continue
            for to_n, to in enumerate((by_x, by_y, (y, oc, x))):
                copy = ib_copy(m, own, ib_s.at[m, to_n], *to)
                copy.start()
                ib_copies.append(copy)

    def pt_recv(k):
        j = (me + k) % LAYER
        return remote(pt_all.at[j], pt_all.at[j], pt_s.at[j], pt_r.at[j], layer_dev(j))

    for k in range(1, LAYER):
        pt_recv(k).wait_recv()

    @pl.when(mid == 0)
    def _():
        text_dir_copy(1).start()

    share = pt_all.shape[2]
    turned_all = jnp.concatenate([pt_all[j].reshape(LINE * share, rows) for j in range(LAYER)], axis=1)

    def weight_copy(k, n):
        t = (z + n) % LINE
        return remote(wp_send.at[k, t], wp_recv.at[k, z], wp_s.at[k, t], wp_r.at[k, z], dev(t, y, c, x))

    pair = (y, oc, x)
    for step in range(len(cuts) + 2):
        m = step
        if m < len(cuts):
            for n, slot in enumerate((by_x, by_y)):
                ib_copy(m, slot, ib_f.at[m, n], *pair).wait_recv()
                if m % 2 == n:
                    on = ib_copy(m, slot, ib_d.at[m], *(by_y if n == 0 else by_x))
                    on.start()
                    ib_copies.append(on)
                on = ib_copy(m, slot, ib_f.at[m, n], *pair)
                on.start()
                ib_copies.append(on)
        if m == 1:
            text_dir_merge(3)
        m = step - 1
        if 0 <= m < len(cuts):
            on = ib_copy(m, diagonal, ib_f.at[m, 2], *pair)
            on.wait_recv()
            on.start()
            ib_copies.append(on)
        m = step - 2
        if m < 0:
            continue
        for slot in ((y, oc, x), (oy, oc, x), (y, oc, ox), (oy, oc, ox)):
            ib_copy(m, slot, ib_f.at[m, 0], *pair).wait_recv()
        k = m - 2
        if k < 0:
            continue
        product = jnp.dot(turned_all, ib_all[k].reshape(LAYER * rows, part), preferred_element_type=F32)
        for t in range(LINE):
            weight_own[k, t] = product[t * share : (t + 1) * share]
            wp_send[k, t] = product[t * share : (t + 1) * share].astype(BF16)
        for n in range(1, LINE):
            weight_copy(k, n).start()

    text_dir_wait(0)
    text_dir_wait(1)
    total = td_own[...] + td_recv[0].astype(F32) + td_recv[1].astype(F32)
    unit = text_unit[...]
    text_out[...] = (total - unit * jnp.sum(unit * total, axis=-1, keepdims=True)) * text_inv

    total = loss_part[q]
    for k, (yy, cc) in enumerate(peers):
        qq = yy * 2 + cc
        remote(loss_recv.at[qq], loss_recv.at[qq], ls_s.at[k], ls_r.at[qq], dev(z, yy, cc, x)).wait_recv()
        total += loss_recv[qq]
    loss_out[...] = total / (LINE * QUAD * rows)

    for k in range(PARTS):
        total = weight_own[k, z]
        for n in range(1, LINE):
            t = (z + n) % LINE
            slot = wp_recv.at[k, t]
            remote(slot, slot, wp_s.at[k, t], wp_r.at[k, t], dev(t, y, c, x)).wait_recv()
            total += wp_recv[k, t].astype(F32)
        weight_out[:, k * part : (k + 1) * part] = total / 64.0

    own_a.wait_send()

    @pl.when(mid == 1)
    def _():
        own_b.wait_send()
        for i in range(1, LINE):
            forward(i).wait_send()

    for copy in pos_copies + image_copies + [image_pass] + id_copies + far_copies + loss_copies:
        copy.wait_send()
    for copy in ib_copies:
        copy.wait_send()
    for k in range(1, LAYER):
        pt_copy(k).wait_send()
    for k in range(1, LINE):
        text_dir_copy(k).wait_send()
        for part in range(PARTS):
            weight_copy(part, k).wait_send()


def settle_kernel(loss_in, weight_in, text_in, loss_out, weight_out, text_out):
    loss_out[...] = loss_in[...]
    weight_out[...] = weight_in[...]
    text_out[...] = text_in[...]


def settle(*results):
    in_vmem = pl.BlockSpec(memory_space=pltpu.VMEM)
    return pl.pallas_call(
        settle_kernel,
        out_shape=tuple(jax.ShapeDtypeStruct(r.shape, r.dtype) for r in results),
        in_specs=[in_vmem] * len(results),
        out_specs=(in_vmem,) * len(results),
        compiler_params=pltpu.CompilerParams(vmem_limit_bytes=61 * 2**20),
    )(*results)


def fused(pooled, w_img, text_emb, pos_index, log_scale, bias):
    _, rows, width = pooled.shape
    emb = w_img.shape[1]
    share = width // (LINE * LAYER)
    vmem, dma = pltpu.VMEM, pltpu.SemaphoreType.DMA
    in_vmem = pl.BlockSpec(memory_space=pltpu.VMEM)
    in_hbm = pl.BlockSpec(memory_space=pltpu.HBM)
    in_smem = pl.BlockSpec(memory_space=pltpu.SMEM)
    block = (rows, emb)
    loss, weight, text = pl.pallas_call(
        fused_kernel,
        out_shape=(
            jax.ShapeDtypeStruct((1, rows), F32),
            jax.ShapeDtypeStruct((share, emb), F32),
            jax.ShapeDtypeStruct(block, F32),
        ),
        in_specs=[in_hbm, in_hbm, in_hbm, in_hbm, in_smem, in_smem],
        out_specs=(in_vmem, in_vmem, in_vmem),
        scratch_shapes=[
            vmem((rows, width), BF16),
            vmem((width, emb), BF16),
            vmem(block, BF16),
            vmem((1, rows), jnp.int32),
            vmem((LINE,) + block, BF16),
            vmem((QUAD,) + block, BF16),
            vmem((QUAD, 1, rows), jnp.int32),
            vmem((LAYER, LINE, share, rows), BF16),
            vmem((LAYER, LINE, share, rows), BF16),
            vmem(block, F32),
            vmem(block, F32),
            vmem(block, F32),
            vmem((2,) + block, F32),
            vmem((LINE,) + block, BF16),
            vmem((LINE,) + block, BF16),
            vmem((QUAD,) + block, F32),
            vmem((2,) + block, BF16),
            vmem((2,) + block, BF16),
            vmem(block, BF16),
            vmem(block, BF16),
            vmem((QUAD, rows, rows), BF16),
            vmem((QUAD, 1, rows), F32),
            vmem((QUAD, 1, rows), F32),
            vmem((PARTS, LAYER, rows, emb // PARTS), BF16),
            vmem((PARTS, LINE, share, emb // PARTS), F32),
            vmem((PARTS, LINE, share, emb // PARTS), BF16),
            vmem((PARTS, LINE, share, emb // PARTS), BF16),
            dma((4,)),
            dma((2,)), dma((LINE,)), dma((LINE,)),
            dma((3,)), dma((QUAD,)),
            dma((3,)), dma((QUAD,)),
            dma((LAYER,)), dma((LAYER,)),
            dma((LINE,)), dma((LINE,)),
            dma((4,)), dma((4,)),
            dma((3,)), dma((QUAD,)),
            dma((PARTS + 2, 3)), dma((PARTS + 2, 3)), dma((PARTS + 2,)), dma((PARTS + 2, LAYER)),
            dma((PARTS, LINE)), dma((PARTS, LINE)),
        ],
        compiler_params=pltpu.CompilerParams(
            collective_id=0, has_side_effects=True, vmem_limit_bytes=63 * 2**20
        ),
    )(pooled[0], w_img, text_emb[0], pos_index, log_scale, bias)
    loss, weight, text = settle(loss, weight, text)
    return loss, weight, text[None]


def normalize(rows):
    squares = jnp.sum(rows * rows, axis=-1, keepdims=True)
    inverse = lax.rsqrt(squares + 1e-06)
    return (rows * inverse, inverse)


def pair_terms(left, right, left_pos, right_start, scale_value, shift):
    logits = scale_value * jnp.dot(left, right.T, preferred_element_type=jnp.float32) + shift
    columns = right_start + jnp.arange(right.shape[0], dtype=jnp.int32)
    sign = jnp.where(left_pos[:, None] == columns[None, :], 1.0, -1.0).astype(jnp.float32)
    losses = jax.nn.softplus(-sign * logits)
    coeffs = (-sign * jax.nn.sigmoid(-sign * logits) * scale_value).astype(jnp.bfloat16)
    return (jnp.sum(losses, axis=1), coeffs)


def transpose_dot(coeffs, rows):
    return lax.dot_general(
        coeffs, rows, (((0,), (0,)), ((), ())), preferred_element_type=jnp.float32
    )


def plain(pooled, w_img, text_emb, pos_index, log_scale, bias):
    scale_value = jnp.exp(log_scale[0])
    shift = bias[0]
    features = pooled[0]
    my_pos = pos_index[0]
    row_count = features.shape[0]
    group_size = row_count * lax.axis_size("blk")
    my_start = lax.axis_index("blk") * row_count
    projected = jnp.dot(features, w_img, preferred_element_type=jnp.float32)
    image_unit, image_inv = normalize(projected)
    image_low = image_unit.astype(jnp.bfloat16)
    text_unit, text_inv = normalize(text_emb[0].astype(jnp.float32))
    text_low = text_unit.astype(jnp.bfloat16)
    piece = lax.all_gather(text_low, "blk", axis=0, tiled=True)
    row_sums, coeffs = pair_terms(image_low, piece, my_pos, jnp.int32(0), scale_value, shift)
    loss_total = row_sums
    image_dir = jnp.dot(coeffs, piece, preferred_element_type=jnp.float32)
    pieces = (
        lax.all_gather(image_low, "blk", axis=0, tiled=True),
        lax.all_gather(my_pos, "blk", axis=0, tiled=True),
    )
    row_sums, coeffs = pair_terms(pieces[0], text_low, pieces[1], my_start, scale_value, shift)
    text_dir = transpose_dot(coeffs, pieces[0])
    image_back = (
        (image_dir - image_unit * jnp.sum(image_unit * image_dir, axis=-1, keepdims=True))
        * image_inv
    ).astype(jnp.bfloat16)
    text_back = (
        text_dir - text_unit * jnp.sum(text_unit * text_dir, axis=-1, keepdims=True)
    ) * text_inv
    weight_part = transpose_dot(features, image_back)
    weight_sum = lax.psum_scatter(weight_part, ("blk", "rep"), scatter_dimension=0, tiled=True)
    return ((loss_total / group_size)[None], weight_sum / 64.0, text_back[None])


def solution(mesh):
    def shards(pooled, w_img, text_emb, pos_index, log_scale, bias):
        _, rows, width = pooled.shape
        fits = mesh.shape["blk"] == LINE * QUAD and mesh.shape["rep"] * QUAD == LAYER
        fits = fits and rows % 128 == 0 and width % (LINE * LAYER * 16) == 0
        return (fused if fits else plain)(pooled, w_img, text_emb, pos_index, log_scale, bias)

    return jax.shard_map(
        shards,
        mesh=mesh,
        in_specs=(P("rep", "blk", None), P(), P("rep", "blk", None), P("rep", "blk"), P(), P()),
        out_specs=(P("rep", "blk"), P(("blk", "rep"), None), P("rep", "blk", None)),
        check_vma=False,
    )
```
